32 devices in a mesh: occ: 4 (over y, core), vir: 8 (over z, x).
Axes of the slice: x: 2, y: 2, z: 4, core: 2. Of those that a mesh axis runs over, the one named last changes fastest.
Arguments:
- amplitudes: bfloat16 [8, 1024, 1024], P('occ', 'vir'), may hold values from -6 to 6
- factors: bfloat16 [24, 1024, 1024], P('vir'), may hold values from -0.0625 to 0.0625
- occ_energy: float32 [100], replicated, may hold values from -2 to -0.3
- vir_energy: float32 [1024], replicated, may hold values from 0.3 to 4
- occ_irrep: int32 [100], replicated, may hold values from 0 to 7
- vir_irrep: int32 [1024], replicated, may hold values from 0 to 7
- pair_orbitals: int32 [8, 2], replicated, may hold values from 0 to 99, as said below
Outputs:
- update: float32 [8, 1024, 1024], P('occ', 'vir')
The draws below stay inside these ranges and needn't reach their ends.
Inputs may be any that keep to these rules, and one draw needn't show every extreme that they name: `pair_orbitals`: pair p + 4 is pair p with i and j swapped; the orbitals named by the first 4 pairs are all distinct.
All inputs are finite; a program needn't handle non-finite values.
Results may differ from the reference program's by a relative error of at most 0.0029.
Values may be sent and summed in bfloat16 or wider, within the bound.
No kernel may reach another device: no remote copies, remote signals or barrier semaphores. Data moves between devices by JAX's collectives and lax.ppermute only.
A program may use at most 128 MiB of HBM per device.

```python
import jax
import jax.numpy as jnp
from jax import lax

V = 1024
NOCC = 100
PAIRS = 8
NAUX = 24


def draw_pair_orbitals(key, part):
    inner = 1 + jax.random.permutation(jax.random.fold_in(key, 11), NOCC - 2)
    ends = jnp.array([0, NOCC - 1], dtype=jnp.int32)
    chosen = jnp.concatenate([ends, inner[:PAIRS - 2].astype(jnp.int32)], axis=0)
    mixing = jax.random.permutation(jax.random.fold_in(key, 23), PAIRS)
    chosen = chosen[mixing]
    half_pairs = PAIRS // 2
    first_orb = chosen[:half_pairs]
    second_orb = chosen[half_pairs:PAIRS]
    upper = jnp.stack([first_orb, second_orb], axis=1)
    lower = jnp.stack([second_orb, first_orb], axis=1)
    return jnp.concatenate([upper, lower], axis=0).astype(jnp.int32)


def plant(entries, own_key, least, high):
    longest = entries.shape.index(max(entries.shape))
    spots = []
    for shift in (0, 1):
        where = [jax.random.randint(jax.random.fold_in(own_key, axis), (), 0, length) for axis, length in enumerate(entries.shape)]
        where[longest] = (where[longest] + shift) % entries.shape[longest]
        spots.append(tuple(where))
    return entries.at[spots[0]].set(least).at[spots[1]].set(high)


def levels(rng, shape, cuts, smallest, high):
    loudness = 1.0
    for position, parts in cuts:
        draws = jax.random.uniform(jax.random.fold_in(jax.random.fold_in(rng, 6), position), (parts,), jnp.float32, smallest / len(cuts), high / len(cuts))
        loudness = loudness * jnp.repeat(jnp.exp(draws), shape[position] // parts).reshape((-1,) + (1,) * (len(shape) - 1 - position))
    return loudness


def centred(rng, shape, deviation, reach, split=(), held_as=jnp.bfloat16):
    values = jax.random.normal(rng, shape, jnp.float32) * deviation
    if len(split) > 0:
        values = levels(rng, shape, split, -0.22, 0.18) * values
    return jnp.clip(values, min=-reach, max=reach).astype(held_as)


def setup_inputs(seed: int = 0) -> dict:
    arg_keys = jax.random.split(jax.random.key(seed), 8)
    return {
        "amplitudes": centred(arg_keys[0], (PAIRS, V, V), 1.0, 6.0, ((0, 4), (1, 8))),
        "factors": centred(arg_keys[1], (NAUX, V, V), (V * 10) ** -0.5, 0.0625, ((0, 8),)),
        "occ_energy": jnp.clip(jax.random.uniform(arg_keys[2], (NOCC,), jnp.float32, -2.0, -0.3), -2.0, -0.3),
        "vir_energy": jnp.clip(jax.random.uniform(arg_keys[3], (V,), jnp.float32, 0.3, 4.0), 0.3, 4.0),
        "occ_irrep": plant(jax.random.randint(arg_keys[4], (NOCC,), 0, 8), jax.random.fold_in(arg_keys[4], 1), 0, 7).astype(jnp.int32),
        "vir_irrep": plant(jax.random.randint(arg_keys[5], (V,), 0, 8), jax.random.fold_in(arg_keys[5], 1), 0, 7).astype(jnp.int32),
        "pair_orbitals": draw_pair_orbitals(jax.random.fold_in(arg_keys[7], 71), 0),
    }


def reference(amplitudes, factors, occ_energy, vir_energy, occ_irrep, vir_irrep, pair_orbitals):
    amp_values = amplitudes.astype(jnp.float32)
    highest = lax.Precision.HIGHEST

    def add_vector(running, factor):
        fac_values = factor.astype(jnp.float32)
        halves = jnp.einsum('pcd,bd->pcb', amp_values, fac_values, precision=highest)
        halves = lax.optimization_barrier(halves.astype(jnp.bfloat16)).astype(jnp.float32)
        ladder = jnp.einsum('ac,pcb->pab', fac_values, halves, precision=highest)
        return running + ladder, None

    summed, _ = lax.scan(add_vector, jnp.zeros((PAIRS, V, V), jnp.float32), factors)
    partner = jnp.transpose(jnp.roll(summed, PAIRS // 2, axis=0), (0, 2, 1))
    first_orb = pair_orbitals[:, 0]
    second_orb = pair_orbitals[:, 1]
    pair_energy = occ_energy[first_orb] + occ_energy[second_orb]
    denominator = vir_energy[None, :, None] + vir_energy[None, None, :] - pair_energy[:, None, None]
    pair_sym = jnp.bitwise_xor(occ_irrep[first_orb], occ_irrep[second_orb])
    combined = jnp.bitwise_xor(jnp.bitwise_xor(pair_sym[:, None, None], vir_irrep[None, :, None]), vir_irrep[None, None, :])
    allowed = combined == 0
    return jnp.where(allowed, (summed + partner) / denominator, jnp.float32(0.0))
```

```python
import functools

import jax
import jax.numpy as jnp
from jax import lax
from jax.experimental import pallas as pl
from jax.experimental.pallas import tpu as pltpu
from jax.sharding import PartitionSpec as P

GROUP_ROWS = 256
ROW_CHUNK = 256


def dot_nt(left, right):
    return lax.dot_general(left, right, (((1,), (1,)), ((), ())), preferred_element_type=jnp.float32)


def ladder_kernel(kept_count, swapped_count, factor_count, has_total, place_ref, factor_ref, *refs):
    block_count = kept_count + swapped_count
    pair_refs = refs[: 2 * block_count]
    rest = refs[2 * block_count :]
    total_ref = rest[0] if has_total else None
    out_ref, rows_ref, left_ref, right_ref = rest[1:] if has_total else rest
    step = pl.program_id(0)
    size = factor_ref.shape[1]
    half = pair_refs[0].shape[0]
    width = block_count * GROUP_ROWS

    @pl.when(step == 0)
    def _():
        flip = place_ref[0]
        for block in range(block_count):
            first = block * GROUP_ROWS + flip * half
            second = block * GROUP_ROWS + (1 - flip) * half
            rows_ref[pl.ds(pl.multiple_of(first, half), half), :] = pair_refs[2 * block][...]
            rows_ref[pl.ds(pl.multiple_of(second, half), half), :] = pair_refs[2 * block + 1][...]

    for number in range(factor_count):

        @pl.when(step == number)
        def _():
            for chunk in range(size // ROW_CHUNK):
                here = pl.ds(chunk * ROW_CHUNK, ROW_CHUNK)
                halves = dot_nt(factor_ref[0, here, :], rows_ref[...]).astype(jnp.bfloat16)
                for block in range(block_count):
                    column = pl.multiple_of(place_ref[1 + block] * GROUP_ROWS, GROUP_ROWS)
                    taken = factor_ref[0, here, pl.ds(column, GROUP_ROWS)]
                    made = halves[:, block * GROUP_ROWS : (block + 1) * GROUP_ROWS]
                    target = pl.ds(number * width + block * GROUP_ROWS, GROUP_ROWS)
                    left_ref[here, target] = taken if block < kept_count else made
                    right_ref[here, target] = made if block < kept_count else taken

    @pl.when(step >= factor_count)
    def _():
        first = pl.multiple_of((step - factor_count) * ROW_CHUNK, ROW_CHUNK)
        product = dot_nt(left_ref[pl.ds(first, ROW_CHUNK), :], right_ref[...])
        out_ref[...] = product + total_ref[...] if has_total else product


def ladder(place, factors, kept, swapped, total):
    factor_count, size, _ = factors.shape
    pairs = list(kept) + list(swapped)
    width = len(pairs) * GROUP_ROWS
    chunk_count = size // ROW_CHUNK

    def factor_map(step, place_ref):
        return (jnp.minimum(step, factor_count - 1), 0, 0)

    def chunk_map(step, place_ref):
        return (jnp.maximum(step - factor_count, 0), 0)

    def whole_map(step, place_ref):
        return (0, 0)

    operands = [factors] + [half for pair in pairs for half in pair]
    in_specs = [pl.BlockSpec((1, size, size), factor_map)]
    in_specs += [pl.BlockSpec(half.shape, whole_map) for half in operands[1:]]
    if total is not None:
        operands.append(total)
        in_specs.append(pl.BlockSpec((ROW_CHUNK, size), chunk_map))
    return pl.pallas_call(
        functools.partial(ladder_kernel, len(kept), len(swapped), factor_count, total is not None),
        out_shape=jax.ShapeDtypeStruct((size, size), jnp.float32),
        grid_spec=pltpu.PrefetchScalarGridSpec(
            num_scalar_prefetch=1,
            grid=(factor_count + chunk_count,),
            in_specs=in_specs,
            out_specs=pl.BlockSpec((ROW_CHUNK, size), chunk_map),
            scratch_shapes=[
                pltpu.VMEM((width, size), jnp.bfloat16),
                pltpu.VMEM((size, factor_count * width), jnp.bfloat16),
                pltpu.VMEM((size, factor_count * width), jnp.bfloat16),
            ],
        ),
        compiler_params=pltpu.CompilerParams(vmem_limit_bytes=40 * 1024 * 1024),
        cost_estimate=pl.CostEstimate(
            flops=4 * factor_count * width * size * size,
            bytes_accessed=2 * factor_count * size * size + 8 * size * size + 2 * width * size,
            transcendentals=0,
        ),
    )(place, *operands)


def per_device(amplitudes, factors, occ_energy, vir_energy, occ_irrep, vir_irrep, pair_orbitals):
    local_pairs, row_count, size = amplitudes.shape
    occ_total = occ_energy.shape[0]
    occ_devices = lax.axis_size("occ")
    vir_devices = lax.axis_size("vir")
    inner = GROUP_ROWS // row_count
    outer = vir_devices // inner
    assert local_pairs == 2 and outer == 4 and inner * row_count == GROUP_ROWS
    occ_index = lax.axis_index("occ")
    vir_index = lax.axis_index("vir")
    z_index = vir_index // inner
    x_index = vir_index % inner
    side = occ_index // (occ_devices // 2)
    across = occ_devices // 2

    def z_swap(block, distance):
        route = [(i, (i // inner ^ distance) * inner + i % inner) for i in range(vir_devices)]
        return lax.ppermute(block, "vir", route)

    def y_swap(block):
        return lax.ppermute(block, "occ", [(i, (i + across) % occ_devices) for i in range(occ_devices)])

    inner_groups = [[g * inner + i for i in range(inner)] for g in range(outer)]

    def x_swap(block):
        return lax.ppermute(block, "vir", [(i, i ^ 1) for i in range(vir_devices)])

    def x_gather(blocks):
        if inner == 2:
            joined = blocks[0] if len(blocks) == 1 else jnp.concatenate(blocks, axis=0)
            came = x_swap(joined)
            return [(b, came[i * row_count : (i + 1) * row_count]) for i, b in enumerate(blocks)]
        pairs = []
        for block in blocks:
            whole = lax.all_gather(block, "vir", axis_index_groups=inner_groups, axis=0, tiled=True)
            pairs.append((whole[: GROUP_ROWS // 2], whole[GROUP_ROWS // 2 :]))
        return pairs

    def x_scatter(sums):
        if inner == 2:
            sent = lax.dynamic_index_in_dim(sums, 1 - x_index, 1, keepdims=False).astype(jnp.bfloat16)
            own = lax.dynamic_index_in_dim(sums, x_index, 1, keepdims=False)
            return own + x_swap(sent).astype(jnp.float32)
        return lax.psum_scatter(sums, "vir", scatter_dimension=1, axis_index_groups=inner_groups)

    def z_scatter(sums, axis, distance, bit):
        sent = lax.dynamic_index_in_dim(sums, 1 - bit, axis, keepdims=False).astype(jnp.bfloat16)
        own = lax.dynamic_index_in_dim(sums, bit, axis, keepdims=False)
        return own + z_swap(sent, distance).astype(jnp.float32)

    z_high = z_index // 2
    z_low = z_index % 2

    kept_0 = lax.dynamic_index_in_dim(amplitudes, side, 0, keepdims=False)
    given = lax.dynamic_index_in_dim(amplitudes, 1 - side, 0, keepdims=False)
    swapped_0 = y_swap(given)
    kept_2 = z_swap(kept_0, 2)
    swapped_2 = z_swap(swapped_0, 2)
    kept_13 = z_swap(jnp.concatenate([kept_0, kept_2], axis=0), 1)
    swapped_13 = z_swap(jnp.concatenate([swapped_0, swapped_2], axis=0), 1)
    kept_1, kept_3 = kept_13[:row_count], kept_13[row_count:]
    swapped_1, swapped_3 = swapped_13[:row_count], swapped_13[row_count:]

    (kept_pair_0,) = x_gather([kept_0])
    (swapped_pair_0,) = x_gather([swapped_0])
    (kept_pair_2,) = x_gather([kept_2])
    (swapped_pair_2,) = x_gather([swapped_2])
    kept_pair_1, kept_pair_3 = x_gather([kept_1, kept_3])
    swapped_pair_1, swapped_pair_3 = x_gather([swapped_1, swapped_3])

    flip = x_index if inner == 2 else jnp.int32(0)

    def place(*zs):
        return jnp.stack([flip, *[z_index ^ d for d in zs]]).astype(jnp.int32)

    total = ladder(place(0, 0), factors, [kept_pair_0], [swapped_pair_0], None)
    total = ladder(place(2, 2), factors, [kept_pair_2], [swapped_pair_2], total)
    total = ladder(place(1, 3), factors, [kept_pair_1, kept_pair_3], [], total)
    total = ladder(place(1, 3), factors, [], [swapped_pair_1, swapped_pair_3], total)

    middle = size // 2
    left = total[:, :middle].reshape(4, inner, row_count, middle)
    left = x_scatter(left)
    left = z_scatter(left.reshape(2, 2, row_count, middle), 1, 1, z_low)
    right = total[:, middle:].reshape(2, 2, GROUP_ROWS, middle)
    right = z_scatter(right, 1, 1, z_low)
    right = x_scatter(right.reshape(2, inner, row_count, middle))
    own_rows = z_scatter(jnp.concatenate([left, right], axis=2), 0, 2, z_high)

    packed = own_rows.astype(jnp.bfloat16).reshape(row_count, vir_devices, row_count)
    packed = jnp.transpose(packed, (1, 2, 0))
    if vir_devices == 8:
        def flipped(blocks):
            blocks = blocks.reshape(2, 2, 2, row_count, row_count)
            for axis in range(3):
                bit = (vir_index >> (2 - axis)) & 1
                blocks = jnp.where(bit == 1, jnp.flip(blocks, axis), blocks)
            return blocks.reshape(8, row_count, row_count)

        turned = flipped(packed)
        came = []
        for step in range(vir_devices):
            route = [
                (o * vir_devices + i, ((o + across) % occ_devices) * vir_devices + (i ^ step))
                for o in range(occ_devices)
                for i in range(vir_devices)
            ]
            came.append(lax.ppermute(turned[step], ("occ", "vir"), route))
        partner = flipped(jnp.stack(came))
    else:
        partner = y_swap(lax.all_to_all(packed, "vir", 0, 0))
    partner = jnp.transpose(partner, (1, 0, 2)).reshape(row_count, size).astype(jnp.float32)

    first = jnp.where(side == 0, own_rows, partner)
    second = jnp.where(side == 0, partner, own_rows)
    numerator = jnp.stack([first, second])

    pair_ids = lax.dynamic_slice_in_dim(pair_orbitals, occ_index * local_pairs, local_pairs, 0)
    row_start = vir_index * row_count
    energy_rows = lax.dynamic_slice_in_dim(vir_energy, row_start, row_count, 0)
    irrep_rows = lax.dynamic_slice_in_dim(vir_irrep, row_start, row_count, 0)
    positions = jnp.arange(occ_total, dtype=jnp.int32)
    first_hot = positions[None, :] == pair_ids[:, 0:1]
    second_hot = positions[None, :] == pair_ids[:, 1:2]
    pair_energy = jnp.sum(jnp.where(first_hot, occ_energy[None, :], 0.0), axis=1) + jnp.sum(
        jnp.where(second_hot, occ_energy[None, :], 0.0), axis=1
    )
    first_irrep = jnp.sum(jnp.where(first_hot, occ_irrep[None, :], 0), axis=1)
    second_irrep = jnp.sum(jnp.where(second_hot, occ_irrep[None, :], 0), axis=1)
    pair_sym = jnp.bitwise_xor(first_irrep, second_irrep)
    combined = jnp.bitwise_xor(
        jnp.bitwise_xor(pair_sym[:, None, None], irrep_rows[None, :, None]),
        vir_irrep[None, None, :],
    )
    allowed = combined == 0
    denominator = (
        energy_rows[None, :, None] + vir_energy[None, None, :] - pair_energy[:, None, None]
    )
    return jnp.where(allowed, numerator / denominator, jnp.float32(0.0))


def solution(mesh):
    return jax.shard_map(
        per_device,
        mesh=mesh,
        in_specs=(P("occ", "vir", None), P("vir", None, None), P(), P(), P(), P(), P()),
        out_specs=P("occ", "vir", None),
        check_vma=False,
    )
```

```python
import functools

import jax
import jax.numpy as jnp
from jax import lax
from jax.experimental import pallas as pl
from jax.experimental.pallas import tpu as pltpu
from jax.sharding import PartitionSpec as P

GROUP_ROWS = 256
ROW_CHUNK = 256


def dot_nt(left, right):
    return lax.dot_general(left, right, (((1,), (1,)), ((), ())), preferred_element_type=jnp.float32)


def ladder_kernel(kept_count, swapped_count, has_total, splits, place_ref, factor_ref, *refs):
    block_count = kept_count + swapped_count
    pair_refs, refs = refs[: 2 * block_count], refs[2 * block_count :]
    total_ref = None
    if has_total:
        total_ref, refs = refs[0], refs[1:]
    out_count = 4 if splits else 1
    out_refs, refs = refs[:out_count], refs[out_count:]
    factors_ref, total_buffer, rows_ref, left_ref, right_ref, factor_sem, total_sem, out_sem = refs[:8]
    factor_count, size, _ = factors_ref.shape
    half = pair_refs[0].shape[0]
    width = block_count * GROUP_ROWS
    chunk_count = size // ROW_CHUNK
    chunks = [pl.ds(c * ROW_CHUNK, ROW_CHUNK) for c in range(chunk_count)]

    factor_copies = [
        [
            pltpu.make_async_copy(factor_ref.at[q, here], factors_ref.at[q, here], factor_sem.at[q, c])
            for c, here in enumerate(chunks)
        ]
        for q in range(factor_count)
    ]
    for copies in factor_copies:
        for copy in copies:
            copy.start()
    if has_total:
        total_copies = [
            pltpu.make_async_copy(total_ref.at[here], total_buffer.at[here], total_sem.at[c])
            for c, here in enumerate(chunks)
        ]
        for copy in total_copies:
            copy.start()

    flip = place_ref[0]
    for block in range(block_count):
        first = block * GROUP_ROWS + flip * half
        second = block * GROUP_ROWS + (1 - flip) * half
        rows_ref[pl.ds(pl.multiple_of(first, half), half), :] = pair_refs[2 * block][...]
        rows_ref[pl.ds(pl.multiple_of(second, half), half), :] = pair_refs[2 * block + 1][...]

    if splits:
        x_index, z_low = place_ref[1 + block_count], place_ref[2 + block_count]
        other_left_ref = refs[8]
    for q in range(factor_count):
        for c, here in enumerate(chunks):
            factor_copies[q][c].wait()
            halves = dot_nt(factors_ref[q, here, :], rows_ref[...]).astype(jnp.bfloat16)
            for block in range(block_count):
                column = pl.multiple_of(place_ref[1 + block] * GROUP_ROWS, GROUP_ROWS)
                taken = factors_ref[q, here, pl.ds(column, GROUP_ROWS)]
                made = halves[:, block * GROUP_ROWS : (block + 1) * GROUP_ROWS]
                target = pl.ds(q * width + block * GROUP_ROWS, GROUP_ROWS)
                if block < kept_count:
                    left_value, right_value = taken, made
                else:
                    left_value, right_value = made, taken
                right_ref[here, target] = right_value
                if not splits:
                    left_ref[here, target] = left_value
                    continue
                for x in range(2):
                    first = jnp.where(x_index == x, size // 2, 0) + c * half
                    piece = left_value[x * half : (x + 1) * half]
                    left_ref[pl.ds(pl.multiple_of(first, half), half), target] = piece
                first = jnp.where(z_low == c % 2, size // 2, 0) + (c // 2) * GROUP_ROWS
                other_left_ref[pl.ds(pl.multiple_of(first, GROUP_ROWS), GROUP_ROWS), target] = left_value

    if not splits:
        out_copies = []
        for c, here in enumerate(chunks):
            product = dot_nt(left_ref[here, :], right_ref[...])
            if has_total:
                total_copies[c].wait()
                product = product + total_buffer[here, :]
            total_buffer[here, :] = product
            copy = pltpu.make_async_copy(total_buffer.at[here], out_refs[0].at[here], out_sem.at[c])
            copy.start()
            out_copies.append(copy)
        for copy in out_copies:
            copy.wait()
        return

    for copy in total_copies:
        copy.wait()
    buffers = refs[9:13]
    middle = size // 2
    out_copies = []
    for sent in (True, False):
        for number, source in enumerate((left_ref, other_left_ref)):
            columns = pl.ds(number * middle, middle)
            rows = pl.ds(0 if sent else middle, middle)
            product = dot_nt(source[rows, :], right_ref[columns, :])
            buffer = buffers[number if sent else 2 + number]
            length = half if number == 0 else GROUP_ROWS
            for part in range(middle // length):
                if number == 0:
                    first = part * GROUP_ROWS + jnp.where(x_index == (0 if sent else 1), half, 0)
                else:
                    first = part * 2 * GROUP_ROWS + jnp.where(z_low == (0 if sent else 1), GROUP_ROWS, 0)
                before = total_buffer[pl.ds(pl.multiple_of(first, length), length), columns]
                value = product[part * length : (part + 1) * length] + before
                buffer[part, :, :] = value.astype(buffer.dtype)
            order = number if sent else 2 + number
            copy = pltpu.make_async_copy(buffer, out_refs[order], out_sem.at[order])
            copy.start()
            out_copies.append(copy)
    for copy in out_copies:
        copy.wait()


def ladder(place, factors, kept, swapped, total, splits=False):
    factor_count, size, _ = factors.shape
    pairs = list(kept) + list(swapped)
    width = len(pairs) * GROUP_ROWS
    chunk_count = size // ROW_CHUNK
    middle = size // 2
    half = GROUP_ROWS // 2
    anywhere = pl.BlockSpec(memory_space=pl.ANY)
    whole = pl.BlockSpec(memory_space=pltpu.VMEM)
    operands = [half_block for pair in pairs for half_block in pair]
    in_specs = [pl.BlockSpec(memory_space=pltpu.SMEM), anywhere] + [whole] * len(operands)
    if total is not None:
        operands.append(total)
        in_specs.append(anywhere)
    scratch = [
        pltpu.VMEM((factor_count, size, size), jnp.bfloat16),
        pltpu.VMEM((size, size), jnp.float32),
        pltpu.VMEM((width, size), jnp.bfloat16),
        pltpu.VMEM((size, factor_count * width), jnp.bfloat16),
        pltpu.VMEM((size, factor_count * width), jnp.bfloat16),
        pltpu.SemaphoreType.DMA((factor_count, chunk_count)),
        pltpu.SemaphoreType.DMA((chunk_count,)),
        pltpu.SemaphoreType.DMA((chunk_count,)),
    ]
    out_shape = [jax.ShapeDtypeStruct((size, size), jnp.float32)]
    if splits:
        shapes = [(size // GROUP_ROWS, half, middle), (size // (2 * GROUP_ROWS), GROUP_ROWS, middle)]
        kinds = [(shape, kind) for kind in (jnp.bfloat16, jnp.float32) for shape in shapes]
        scratch.append(pltpu.VMEM((size, factor_count * width), jnp.bfloat16))
        scratch += [pltpu.VMEM(shape, kind) for shape, kind in kinds]
        out_shape = [jax.ShapeDtypeStruct(shape, kind) for shape, kind in kinds]
    out = pl.pallas_call(
        functools.partial(ladder_kernel, len(kept), len(swapped), total is not None, splits),
        out_shape=out_shape,
        in_specs=in_specs,
        out_specs=[anywhere] * len(out_shape),
        scratch_shapes=scratch,
        compiler_params=pltpu.CompilerParams(vmem_limit_bytes=36 * 1024 * 1024),
        cost_estimate=pl.CostEstimate(
            flops=4 * factor_count * width * size * size,
            bytes_accessed=2 * factor_count * size * size + 8 * size * size + 2 * width * size,
            transcendentals=0,
        ),
    )(place, factors, *operands)
    return out if splits else out[0]


def per_device(amplitudes, factors, occ_energy, vir_energy, occ_irrep, vir_irrep, pair_orbitals):
    local_pairs, row_count, size = amplitudes.shape
    occ_total = occ_energy.shape[0]
    occ_devices = lax.axis_size("occ")
    vir_devices = lax.axis_size("vir")
    inner = GROUP_ROWS // row_count
    outer = vir_devices // inner
    assert local_pairs == 2 and outer == 4 and inner * row_count == GROUP_ROWS
    occ_index = lax.axis_index("occ")
    vir_index = lax.axis_index("vir")
    z_index = vir_index // inner
    x_index = vir_index % inner
    side = occ_index // (occ_devices // 2)
    across = occ_devices // 2

    def z_swap(block, distance):
        route = [(i, (i // inner ^ distance) * inner + i % inner) for i in range(vir_devices)]
        return lax.ppermute(block, "vir", route)

    def y_swap(block):
        return lax.ppermute(block, "occ", [(i, (i + across) % occ_devices) for i in range(occ_devices)])

    inner_groups = [[g * inner + i for i in range(inner)] for g in range(outer)]

    def x_swap(block):
        return lax.ppermute(block, "vir", [(i, i ^ 1) for i in range(vir_devices)])

    def x_gather(block):
        if inner == 2:
            return block, x_swap(block)
        whole = lax.all_gather(block, "vir", axis_index_groups=inner_groups, axis=0, tiled=True)
        return whole[: GROUP_ROWS // 2], whole[GROUP_ROWS // 2 :]

    def x_scatter(sums):
        return lax.psum_scatter(sums, "vir", scatter_dimension=1, axis_index_groups=inner_groups)

    def z_scatter(sums, axis, distance, bit):
        sent = lax.dynamic_index_in_dim(sums, 1 - bit, axis, keepdims=False).astype(jnp.bfloat16)
        own = lax.dynamic_index_in_dim(sums, bit, axis, keepdims=False)
        return own + z_swap(sent, distance).astype(jnp.float32)

    def halved(own, came, bit, swap):
        came = came.reshape(own.shape)

        def half(index):
            mine = lax.dynamic_index_in_dim(own, index, 1, keepdims=False)
            theirs = lax.dynamic_index_in_dim(came, index, 1, keepdims=False)
            return mine + theirs.astype(jnp.float32)

        return half(bit) + swap(half(1 - bit).astype(jnp.bfloat16)).astype(jnp.float32)

    z_high = z_index // 2
    z_low = z_index % 2

    kept_0 = lax.dynamic_index_in_dim(amplitudes, side, 0, keepdims=False)
    given = lax.dynamic_index_in_dim(amplitudes, 1 - side, 0, keepdims=False)
    swapped_0 = y_swap(given)
    kept_2 = z_swap(kept_0, 2)
    kept_1 = z_swap(kept_0, 1)
    kept_pair_0 = x_gather(kept_0)
    swapped_2 = z_swap(swapped_0, 2)
    swapped_1 = z_swap(swapped_0, 1)
    swapped_pair_0 = x_gather(swapped_0)
    kept_pair_1 = x_gather(kept_1)
    kept_3 = z_swap(kept_2, 1)
    kept_pair_2 = x_gather(kept_2)
    swapped_pair_1 = x_gather(swapped_1)
    swapped_3 = z_swap(swapped_2, 1)
    swapped_pair_2 = x_gather(swapped_2)
    kept_pair_3 = x_gather(kept_3)
    swapped_pair_3 = x_gather(swapped_3)

    flip = x_index if inner == 2 else jnp.int32(0)

    def place(*zs):
        last = [x_index, z_low]
        return jnp.stack([flip, *[z_index ^ d for d in zs], *last]).astype(jnp.int32)

    total = ladder(place(0), factors, [kept_pair_0], [], None)
    total = ladder(place(1, 0), factors, [kept_pair_1], [swapped_pair_0], total)
    total = ladder(place(2, 1), factors, [kept_pair_2], [swapped_pair_1], total)
    total = ladder(place(3, 2), factors, [kept_pair_3], [swapped_pair_2], total)

    middle = size // 2
    if inner == 2:
        sent_x, sent_z, own_x, own_z = ladder(place(3), factors, [], [swapped_pair_3], total, True)
        left = halved(own_x.reshape(2, 2, row_count, middle), x_swap(sent_x), z_low, lambda b: z_swap(b, 1))
        right = halved(own_z.reshape(2, 2, row_count, middle), z_swap(sent_z, 1), x_index, x_swap)
    else:
        total = ladder(place(3), factors, [], [swapped_pair_3], total)
        left = x_scatter(total[:, :middle].reshape(4, inner, row_count, middle))
        left = z_scatter(left.reshape(2, 2, row_count, middle), 1, 1, z_low)
        right = z_scatter(total[:, middle:].reshape(2, 2, GROUP_ROWS, middle), 1, 1, z_low)
        right = x_scatter(right.reshape(2, inner, row_count, middle))
    own_rows = jnp.concatenate([z_scatter(left, 0, 2, z_high), z_scatter(right, 0, 2, z_high)], axis=1)

    packed = own_rows.astype(jnp.bfloat16).reshape(row_count, vir_devices, row_count)
    packed = jnp.transpose(packed, (1, 2, 0))
    if inner == 2:
        def flipped(blocks):
            blocks = blocks.reshape(2, 2, *blocks.shape[1:])
            blocks = jnp.where(z_high == 1, jnp.flip(blocks, 0), blocks)
            blocks = jnp.where(z_low == 1, jnp.flip(blocks, 1), blocks)
            return blocks.reshape(4, *blocks.shape[2:])

        packed = packed.reshape(4, 2, row_count, row_count)
        stays = lax.dynamic_index_in_dim(packed, x_index, 1, keepdims=False)
        leaves = lax.dynamic_index_in_dim(packed, 1 - x_index, 1, keepdims=False)
        came = x_swap(leaves)
        first = jnp.where(x_index == 0, stays, came)
        second = jnp.where(x_index == 0, came, stays)
        turned = flipped(jnp.concatenate([first, second], axis=2))
        came = []
        for step in range(4):
            route = [
                (o * vir_devices + i, ((o + across) % occ_devices) * vir_devices + (i ^ 2 * step))
                for o in range(occ_devices)
                for i in range(vir_devices)
            ]
            came.append(lax.ppermute(turned[step], ("occ", "vir"), route))
        partner = flipped(jnp.stack(came))
    else:
        partner = y_swap(lax.all_to_all(packed, "vir", 0, 0))
    partner = jnp.transpose(partner, (1, 0, 2)).reshape(row_count, size).astype(jnp.float32)

    first = jnp.where(side == 0, own_rows, partner)
    second = jnp.where(side == 0, partner, own_rows)
    numerator = jnp.stack([first, second])

    pair_ids = lax.dynamic_slice_in_dim(pair_orbitals, occ_index * local_pairs, local_pairs, 0)
    row_start = vir_index * row_count
    energy_rows = lax.dynamic_slice_in_dim(vir_energy, row_start, row_count, 0)
    irrep_rows = lax.dynamic_slice_in_dim(vir_irrep, row_start, row_count, 0)
    positions = jnp.arange(occ_total, dtype=jnp.int32)
    first_hot = positions[None, :] == pair_ids[:, 0:1]
    second_hot = positions[None, :] == pair_ids[:, 1:2]
    pair_energy = jnp.sum(jnp.where(first_hot, occ_energy[None, :], 0.0), axis=1) + jnp.sum(
        jnp.where(second_hot, occ_energy[None, :], 0.0), axis=1
    )
    first_irrep = jnp.sum(jnp.where(first_hot, occ_irrep[None, :], 0), axis=1)
    second_irrep = jnp.sum(jnp.where(second_hot, occ_irrep[None, :], 0), axis=1)
    pair_sym = jnp.bitwise_xor(first_irrep, second_irrep)
    combined = jnp.bitwise_xor(
        jnp.bitwise_xor(pair_sym[:, None, None], irrep_rows[None, :, None]),
        vir_irrep[None, None, :],
    )
    allowed = combined == 0
    denominator = (
        energy_rows[None, :, None] + vir_energy[None, None, :] - pair_energy[:, None, None]
    )
    return jnp.where(allowed, numerator / denominator, jnp.float32(0.0))


def solution(mesh):
    return jax.shard_map(
        per_device,
        mesh=mesh,
        in_specs=(P("occ", "vir", None), P("vir", None, None), P(), P(), P(), P(), P()),
        out_specs=P("occ", "vir", None),
        check_vma=False,
    )
```

```python
import functools

import jax
import jax.numpy as jnp
from jax import lax
from jax.experimental import pallas as pl
from jax.experimental.pallas import tpu as pltpu
from jax.sharding import PartitionSpec as P

GROUP_ROWS = 256


def dot_nt(left, right):
    return lax.dot_general(left, right, (((1,), (1,)), ((), ())), preferred_element_type=jnp.float32)


def ladder_kernel(distances, inner, kept_count, has_total, splits, factor_ref, *refs):
    block_count = len(distances)
    vir_index = lax.axis_index("vir")
    z_index = vir_index // inner
    x_index = vir_index % inner
    z_low = z_index % 2
    pair_refs, refs = refs[: 2 * block_count], refs[2 * block_count :]
    total_ref = None
    if has_total:
        total_ref, refs = refs[0], refs[1:]
    out_count = 4 if splits else 1
    out_refs, refs = refs[:out_count], refs[out_count:]
    rows_ref, left_ref, right_ref = refs[:3]
    factor_count, size, _ = factor_ref.shape
    half = pair_refs[0].shape[0]
    width = block_count * GROUP_ROWS

    flip = x_index if inner == 2 else 0
    for block in range(block_count):
        first = block * GROUP_ROWS + flip * half
        second = block * GROUP_ROWS + (1 - flip) * half
        rows_ref[pl.ds(pl.multiple_of(first, half), half), :] = pair_refs[2 * block][...]
        rows_ref[pl.ds(pl.multiple_of(second, half), half), :] = pair_refs[2 * block + 1][...]

    if splits:
        other_left_ref = refs[3]
    for q in range(factor_count):
        if block_count == 1:
            halves = dot_nt(rows_ref[...], factor_ref[q]).T.astype(jnp.bfloat16)
        else:
            halves = dot_nt(factor_ref[q], rows_ref[...]).astype(jnp.bfloat16)
        for block in range(block_count):
            column = pl.multiple_of((z_index ^ distances[block]) * GROUP_ROWS, GROUP_ROWS)
            taken = factor_ref[q, :, pl.ds(column, GROUP_ROWS)]
            made = halves[:, block * GROUP_ROWS : (block + 1) * GROUP_ROWS]
            target = pl.ds(q * width + block * GROUP_ROWS, GROUP_ROWS)
            if block < kept_count:
                left_value, right_value = taken, made
            else:
                left_value, right_value = made, taken
            right_ref[:, target] = right_value
            if not splits:
                left_ref[:, target] = left_value
                continue
            for c in range(size // GROUP_ROWS):
                piece = left_value[c * GROUP_ROWS : (c + 1) * GROUP_ROWS]
                for x in range(2):
                    first = jnp.where(x_index == x, size // 2, 0) + c * half
                    left_ref[pl.ds(pl.multiple_of(first, half), half), target] = piece[x * half : (x + 1) * half]
                first = jnp.where(z_low == c % 2, size // 2, 0) + (c // 2) * GROUP_ROWS
                other_left_ref[pl.ds(pl.multiple_of(first, GROUP_ROWS), GROUP_ROWS), target] = piece

    if not splits:
        product = dot_nt(left_ref[...], right_ref[...])
        out_refs[0][...] = product + total_ref[...] if has_total else product
        return

    middle = size // 2
    for sent in (True, False):
        for number, source in enumerate((left_ref, other_left_ref)):
            columns = pl.ds(number * middle, middle)
            target = out_refs[number if sent else 2 + number]
            length = half if number == 0 else GROUP_ROWS
            product = dot_nt(source[pl.ds(0 if sent else middle, middle), :], right_ref[columns, :])
            for part in range(middle // length):
                if number == 0:
                    first = part * GROUP_ROWS + jnp.where(x_index == (0 if sent else 1), half, 0)
                else:
                    first = part * 2 * GROUP_ROWS + jnp.where(z_low == (0 if sent else 1), GROUP_ROWS, 0)
                before = total_ref[pl.ds(pl.multiple_of(first, length), length), columns]
                value = product[part * length : (part + 1) * length] + before
                target[part, :, :] = value.astype(target.dtype)


def ladder(distances, inner, factors, kept, swapped, total, splits=False):
    factor_count, size, _ = factors.shape
    pairs = list(kept) + list(swapped)
    width = len(pairs) * GROUP_ROWS
    middle = size // 2
    half = GROUP_ROWS // 2
    whole = pl.BlockSpec(memory_space=pltpu.VMEM)
    operands = [half_block for pair in pairs for half_block in pair]
    if total is not None:
        operands.append(total)
    in_specs = [whole] * (1 + len(operands))
    scratch = [
        pltpu.VMEM((width, size), jnp.bfloat16),
        pltpu.VMEM((size, factor_count * width), jnp.bfloat16),
        pltpu.VMEM((size, factor_count * width), jnp.bfloat16),
    ]
    out_shape = [jax.ShapeDtypeStruct((size, size), jnp.float32)]
    if splits:
        shapes = [(size // GROUP_ROWS, half, middle), (size // (2 * GROUP_ROWS), GROUP_ROWS, middle)]
        kinds = [(shape, kind) for kind in (jnp.bfloat16, jnp.float32) for shape in shapes]
        scratch.append(pltpu.VMEM((size, factor_count * width), jnp.bfloat16))
        out_shape = [jax.ShapeDtypeStruct(shape, kind) for shape, kind in kinds]
    out = pl.pallas_call(
        functools.partial(ladder_kernel, distances, inner, len(kept), total is not None, splits),
        out_shape=out_shape,
        in_specs=in_specs,
        out_specs=[whole] * len(out_shape),
        scratch_shapes=scratch,
        input_output_aliases={} if splits or total is None else {len(operands): 0},
        compiler_params=pltpu.CompilerParams(vmem_limit_bytes=24 * 1024 * 1024),
        cost_estimate=pl.CostEstimate(
            flops=4 * factor_count * width * size * size,
            bytes_accessed=2 * factor_count * size * size + 8 * size * size + 2 * width * size,
            transcendentals=0,
        ),
    )(factors, *operands)
    return out if splits else out[0]


def per_device(amplitudes, factors, occ_energy, vir_energy, occ_irrep, vir_irrep, pair_orbitals):
    local_pairs, row_count, size = amplitudes.shape
    occ_total = occ_energy.shape[0]
    occ_devices = lax.axis_size("occ")
    vir_devices = lax.axis_size("vir")
    inner = GROUP_ROWS // row_count
    outer = vir_devices // inner
    assert local_pairs == 2 and outer == 4 and inner * row_count == GROUP_ROWS
    occ_index = lax.axis_index("occ")
    vir_index = lax.axis_index("vir")
    z_index = vir_index // inner
    x_index = vir_index % inner
    side = occ_index // (occ_devices // 2)
    across = occ_devices // 2

    def z_swap(block, distance):
        route = [(i, (i // inner ^ distance) * inner + i % inner) for i in range(vir_devices)]
        return lax.ppermute(block, "vir", route)

    def y_swap(block):
        return lax.ppermute(block, "occ", [(i, (i + across) % occ_devices) for i in range(occ_devices)])

    inner_groups = [[g * inner + i for i in range(inner)] for g in range(outer)]

    def x_swap(block):
        return lax.ppermute(block, "vir", [(i, i ^ 1) for i in range(vir_devices)])

    def x_gather(block):
        if inner == 2:
            return block, x_swap(block)
        whole = lax.all_gather(block, "vir", axis_index_groups=inner_groups, axis=0, tiled=True)
        return whole[: GROUP_ROWS // 2], whole[GROUP_ROWS // 2 :]

    def x_scatter(sums):
        return lax.psum_scatter(sums, "vir", scatter_dimension=1, axis_index_groups=inner_groups)

    def z_scatter(sums, axis, distance, bit):
        sent = lax.dynamic_index_in_dim(sums, 1 - bit, axis, keepdims=False).astype(jnp.bfloat16)
        own = lax.dynamic_index_in_dim(sums, bit, axis, keepdims=False)
        return own + z_swap(sent, distance).astype(jnp.float32)

    def halved(own, came, bit, swap):
        came = came.reshape(own.shape)

        def half(index):
            mine = lax.dynamic_index_in_dim(own, index, 1, keepdims=False)
            theirs = lax.dynamic_index_in_dim(came, index, 1, keepdims=False)
            return mine + theirs.astype(jnp.float32)

        return half(bit) + swap(half(1 - bit).astype(jnp.bfloat16)).astype(jnp.float32)

    z_high = z_index // 2
    z_low = z_index % 2

    kept_0 = lax.dynamic_index_in_dim(amplitudes, side, 0, keepdims=False)
    given = lax.dynamic_index_in_dim(amplitudes, 1 - side, 0, keepdims=False)
    swapped_0 = y_swap(given)
    kept_2 = z_swap(kept_0, 2)
    kept_1 = z_swap(kept_0, 1)
    kept_pair_0 = x_gather(kept_0)
    swapped_2 = z_swap(swapped_0, 2)
    swapped_1 = z_swap(swapped_0, 1)
    swapped_pair_0 = x_gather(swapped_0)
    kept_pair_1 = x_gather(kept_1)
    total = ladder((0,), inner, factors, [kept_pair_0], [], None)
    kept_2, swapped_1, total = lax.optimization_barrier((kept_2, swapped_1, total))
    kept_3 = z_swap(kept_2, 1)
    kept_pair_2 = x_gather(kept_2)
    swapped_pair_1 = x_gather(swapped_1)
    total = ladder((1, 0), inner, factors, [kept_pair_1], [swapped_pair_0], total)
    swapped_2, kept_3, total = lax.optimization_barrier((swapped_2, kept_3, total))
    swapped_3 = z_swap(swapped_2, 1)
    swapped_pair_2 = x_gather(swapped_2)
    kept_pair_3 = x_gather(kept_3)
    total = ladder((2, 1), inner, factors, [kept_pair_2], [swapped_pair_1], total)
    swapped_3, total = lax.optimization_barrier((swapped_3, total))
    swapped_pair_3 = x_gather(swapped_3)
    total = ladder((3, 2), inner, factors, [kept_pair_3], [swapped_pair_2], total)

    middle = size // 2
    if inner == 2:
        sent_x, sent_z, own_x, own_z = ladder((3,), inner, factors, [], [swapped_pair_3], total, True)
        left = halved(own_x.reshape(2, 2, row_count, middle), x_swap(sent_x), z_low, lambda b: z_swap(b, 1))
        right = halved(own_z.reshape(2, 2, row_count, middle), z_swap(sent_z, 1), x_index, x_swap)
    else:
        total = ladder((3,), inner, factors, [], [swapped_pair_3], total)
        left = x_scatter(total[:, :middle].reshape(4, inner, row_count, middle))
        left = z_scatter(left.reshape(2, 2, row_count, middle), 1, 1, z_low)
        right = z_scatter(total[:, middle:].reshape(2, 2, GROUP_ROWS, middle), 1, 1, z_low)
        right = x_scatter(right.reshape(2, inner, row_count, middle))
    own_rows = jnp.concatenate([z_scatter(left, 0, 2, z_high), z_scatter(right, 0, 2, z_high)], axis=1)

    packed = own_rows.astype(jnp.bfloat16).reshape(row_count, vir_devices, row_count)
    packed = jnp.transpose(packed, (1, 2, 0))
    if inner == 2:
        def flipped(blocks):
            blocks = blocks.reshape(2, 2, *blocks.shape[1:])
            blocks = jnp.where(z_high == 1, jnp.flip(blocks, 0), blocks)
            blocks = jnp.where(z_low == 1, jnp.flip(blocks, 1), blocks)
            return blocks.reshape(4, *blocks.shape[2:])

        packed = packed.reshape(4, 2, row_count, row_count)
        stays = lax.dynamic_index_in_dim(packed, x_index, 1, keepdims=False)
        leaves = lax.dynamic_index_in_dim(packed, 1 - x_index, 1, keepdims=False)
        came = x_swap(leaves)
        first = jnp.where(x_index == 0, stays, came)
        second = jnp.where(x_index == 0, came, stays)
        turned = flipped(jnp.concatenate([first, second], axis=2))
        came = []
        for step in range(4):
            route = [
                (o * vir_devices + i, ((o + across) % occ_devices) * vir_devices + (i ^ 2 * step))
                for o in range(occ_devices)
                for i in range(vir_devices)
            ]
            came.append(lax.ppermute(turned[step], ("occ", "vir"), route))
        partner = flipped(jnp.stack(came))
    else:
        partner = y_swap(lax.all_to_all(packed, "vir", 0, 0))
    partner = jnp.transpose(partner, (1, 0, 2)).reshape(row_count, size).astype(jnp.float32)

    first = jnp.where(side == 0, own_rows, partner)
    second = jnp.where(side == 0, partner, own_rows)
    numerator = jnp.stack([first, second])

    pair_ids = lax.dynamic_slice_in_dim(pair_orbitals, occ_index * local_pairs, local_pairs, 0)
    row_start = vir_index * row_count
    energy_rows = lax.dynamic_slice_in_dim(vir_energy, row_start, row_count, 0)
    irrep_rows = lax.dynamic_slice_in_dim(vir_irrep, row_start, row_count, 0)
    positions = jnp.arange(occ_total, dtype=jnp.int32)
    first_hot = positions[None, :] == pair_ids[:, 0:1]
    second_hot = positions[None, :] == pair_ids[:, 1:2]
    pair_energy = jnp.sum(jnp.where(first_hot, occ_energy[None, :], 0.0), axis=1) + jnp.sum(
        jnp.where(second_hot, occ_energy[None, :], 0.0), axis=1
    )
    first_irrep = jnp.sum(jnp.where(first_hot, occ_irrep[None, :], 0), axis=1)
    second_irrep = jnp.sum(jnp.where(second_hot, occ_irrep[None, :], 0), axis=1)
    pair_sym = jnp.bitwise_xor(first_irrep, second_irrep)
    combined = jnp.bitwise_xor(
        jnp.bitwise_xor(pair_sym[:, None, None], irrep_rows[None, :, None]),
        vir_irrep[None, None, :],
    )
    allowed = combined == 0
    denominator = (
        energy_rows[None, :, None] + vir_energy[None, None, :] - pair_energy[:, None, None]
    )
    return jnp.where(allowed, numerator / denominator, jnp.float32(0.0))


def solution(mesh):
    return jax.shard_map(
        per_device,
        mesh=mesh,
        in_specs=(P("occ", "vir", None), P("vir", None, None), P(), P(), P(), P(), P()),
        out_specs=P("occ", "vir", None),
        check_vma=False,
    )
```

```python
import functools

import jax
import jax.numpy as jnp
from jax import lax
from jax.experimental import pallas as pl
from jax.experimental.pallas import tpu as pltpu
from jax.sharding import PartitionSpec as P

GROUP_ROWS = 256


def dot_nt(left, right):
    return lax.dot_general(left, right, (((1,), (1,)), ((), ())), preferred_element_type=jnp.float32)


def ladder_kernel(distances, inner, kept_count, has_total, splits, loads, factor_ref, *refs):
    block_count = len(distances)
    vir_index = lax.axis_index("vir")
    z_index = vir_index // inner
    x_index = vir_index % inner
    z_low = z_index % 2
    pair_refs, refs = refs[: 2 * block_count], refs[2 * block_count :]
    total_ref = None
    if has_total:
        total_ref, refs = refs[0], refs[1:]
    out_count = 4 if splits else 1
    out_refs, refs = refs[:out_count], refs[out_count:]
    rows_ref, left_ref, right_ref = refs[:3]
    loading = []
    if loads:
        source_ref, factor_ref, factor_sem = factor_ref, refs[0], refs[4]
        out_refs, (rows_ref, left_ref, right_ref) = out_refs, refs[1:4]
        for q in range(factor_ref.shape[0]):
            loading.append(pltpu.make_async_copy(source_ref.at[q], factor_ref.at[q], factor_sem.at[q]))
            loading[q].start()
    factor_count, size, _ = factor_ref.shape
    half = pair_refs[0].shape[0]
    width = block_count * GROUP_ROWS

    flip = x_index if inner == 2 else 0
    for block in range(block_count):
        first = block * GROUP_ROWS + flip * half
        second = block * GROUP_ROWS + (1 - flip) * half
        rows_ref[pl.ds(pl.multiple_of(first, half), half), :] = pair_refs[2 * block][...]
        rows_ref[pl.ds(pl.multiple_of(second, half), half), :] = pair_refs[2 * block + 1][...]

    if splits:
        other_left_ref = refs[3]
    for q in range(factor_count):
        if loads:
            loading[q].wait()
        if block_count == 1:
            halves = dot_nt(rows_ref[...], factor_ref[q]).T.astype(jnp.bfloat16)
        else:
            halves = dot_nt(factor_ref[q], rows_ref[...]).astype(jnp.bfloat16)
        for block in range(block_count):
            column = pl.multiple_of((z_index ^ distances[block]) * GROUP_ROWS, GROUP_ROWS)
            taken = factor_ref[q, :, pl.ds(column, GROUP_ROWS)]
            made = halves[:, block * GROUP_ROWS : (block + 1) * GROUP_ROWS]
            target = pl.ds(q * width + block * GROUP_ROWS, GROUP_ROWS)
            if block < kept_count:
                left_value, right_value = taken, made
            else:
                left_value, right_value = made, taken
            right_ref[:, target] = right_value
            if not splits:
                left_ref[:, target] = left_value
                continue
            for c in range(size // GROUP_ROWS):
                piece = left_value[c * GROUP_ROWS : (c + 1) * GROUP_ROWS]
                for x in range(2):
                    first = jnp.where(x_index == x, size // 2, 0) + c * half
                    left_ref[pl.ds(pl.multiple_of(first, half), half), target] = piece[x * half : (x + 1) * half]
                first = jnp.where(z_low == c % 2, size // 2, 0) + (c // 2) * GROUP_ROWS
                other_left_ref[pl.ds(pl.multiple_of(first, GROUP_ROWS), GROUP_ROWS), target] = piece

    if not splits:
        product = dot_nt(left_ref[...], right_ref[...])
        out_refs[0][...] = product + total_ref[...] if has_total else product
        return

    middle = size // 2
    for sent in (True, False):
        for number, source in enumerate((left_ref, other_left_ref)):
            columns = pl.ds(number * middle, middle)
            target = out_refs[number if sent else 2 + number]
            length = half if number == 0 else GROUP_ROWS
            product = dot_nt(source[pl.ds(0 if sent else middle, middle), :], right_ref[columns, :])
            for part in range(middle // length):
                if number == 0:
                    first = part * GROUP_ROWS + jnp.where(x_index == (0 if sent else 1), half, 0)
                else:
                    first = part * 2 * GROUP_ROWS + jnp.where(z_low == (0 if sent else 1), GROUP_ROWS, 0)
                before = total_ref[pl.ds(pl.multiple_of(first, length), length), columns]
                value = product[part * length : (part + 1) * length] + before
                target[part, :, :] = value.astype(target.dtype)


def ladder(distances, inner, factors, kept, swapped, total, splits=False, loads=False):
    factor_count, size, _ = factors.shape
    pairs = list(kept) + list(swapped)
    width = len(pairs) * GROUP_ROWS
    middle = size // 2
    half = GROUP_ROWS // 2
    whole = pl.BlockSpec(memory_space=pltpu.VMEM)
    operands = [half_block for pair in pairs for half_block in pair]
    if total is not None:
        operands.append(total)
    in_specs = [whole] * (1 + len(operands))
    scratch = [
        pltpu.VMEM((width, size), jnp.bfloat16),
        pltpu.VMEM((size, factor_count * width), jnp.bfloat16),
        pltpu.VMEM((size, factor_count * width), jnp.bfloat16),
    ]
    out_shape = [jax.ShapeDtypeStruct((size, size), jnp.float32)]
    if splits:
        shapes = [(size // GROUP_ROWS, half, middle), (size // (2 * GROUP_ROWS), GROUP_ROWS, middle)]
        kinds = [(shape, kind) for kind in (jnp.bfloat16, jnp.float32) for shape in shapes]
        scratch.append(pltpu.VMEM((size, factor_count * width), jnp.bfloat16))
        out_shape = [jax.ShapeDtypeStruct(shape, kind) for shape, kind in kinds]
    if loads:
        factors = pltpu.with_memory_space_constraint(factors, pltpu.HBM)
        in_specs[0] = pl.BlockSpec(memory_space=pl.ANY)
        out_shape.append(jax.ShapeDtypeStruct(factors.shape, factors.dtype))
        scratch.append(pltpu.SemaphoreType.DMA((factor_count,)))
    out = pl.pallas_call(
        functools.partial(ladder_kernel, distances, inner, len(kept), total is not None, splits, loads),
        out_shape=out_shape,
        in_specs=in_specs,
        out_specs=[whole] * len(out_shape),
        scratch_shapes=scratch,
        input_output_aliases={} if splits or total is None else {len(operands): 0},
        compiler_params=pltpu.CompilerParams(vmem_limit_bytes=24 * 1024 * 1024),
        cost_estimate=pl.CostEstimate(
            flops=4 * factor_count * width * size * size,
            bytes_accessed=2 * factor_count * size * size + 8 * size * size + 2 * width * size,
            transcendentals=0,
        ),
    )(factors, *operands)
    return out if splits or loads else out[0]


def per_device(amplitudes, factors, occ_energy, vir_energy, occ_irrep, vir_irrep, pair_orbitals):
    local_pairs, row_count, size = amplitudes.shape
    occ_total = occ_energy.shape[0]
    occ_devices = lax.axis_size("occ")
    vir_devices = lax.axis_size("vir")
    inner = GROUP_ROWS // row_count
    outer = vir_devices // inner
    assert local_pairs == 2 and outer == 4 and inner * row_count == GROUP_ROWS
    occ_index = lax.axis_index("occ")
    vir_index = lax.axis_index("vir")
    z_index = vir_index // inner
    x_index = vir_index % inner
    side = occ_index // (occ_devices // 2)
    across = occ_devices // 2

    def z_swap(block, distance):
        route = [(i, (i // inner ^ distance) * inner + i % inner) for i in range(vir_devices)]
        return lax.ppermute(block, "vir", route)

    def y_swap(block):
        return lax.ppermute(block, "occ", [(i, (i + across) % occ_devices) for i in range(occ_devices)])

    inner_groups = [[g * inner + i for i in range(inner)] for g in range(outer)]

    def x_swap(block):
        return lax.ppermute(block, "vir", [(i, i ^ 1) for i in range(vir_devices)])

    def x_gather(block):
        if inner == 2:
            return block, x_swap(block)
        whole = lax.all_gather(block, "vir", axis_index_groups=inner_groups, axis=0, tiled=True)
        return whole[: GROUP_ROWS // 2], whole[GROUP_ROWS // 2 :]

    def x_scatter(sums):
        return lax.psum_scatter(sums, "vir", scatter_dimension=1, axis_index_groups=inner_groups)

    def z_scatter(sums, axis, distance, bit):
        sent = lax.dynamic_index_in_dim(sums, 1 - bit, axis, keepdims=False).astype(jnp.bfloat16)
        own = lax.dynamic_index_in_dim(sums, bit, axis, keepdims=False)
        return own + z_swap(sent, distance).astype(jnp.float32)

    def halved(own, came, bit, swap):
        came = came.reshape(own.shape)

        def half(index):
            mine = lax.dynamic_index_in_dim(own, index, 1, keepdims=False)
            theirs = lax.dynamic_index_in_dim(came, index, 1, keepdims=False)
            return mine + theirs.astype(jnp.float32)

        return half(bit) + swap(half(1 - bit).astype(jnp.bfloat16)).astype(jnp.float32)

    z_high = z_index // 2
    z_low = z_index % 2

    kept_0 = lax.dynamic_index_in_dim(amplitudes, side, 0, keepdims=False)
    given = lax.dynamic_index_in_dim(amplitudes, 1 - side, 0, keepdims=False)
    swapped_0 = y_swap(given)
    def step(distance, kept, swapped, total):
        return ladder((distance,), inner, factors, kept, swapped, total)

    after = lax.optimization_barrier
    kept_2 = z_swap(kept_0, 2)
    kept_1 = z_swap(kept_0, 1)
    kept_pair_0 = x_gather(kept_0)
    swapped_2 = z_swap(swapped_0, 2)
    swapped_1 = z_swap(swapped_0, 1)
    swapped_pair_0 = x_gather(swapped_0)
    kept_pair_1 = x_gather(kept_1)
    total, factors = ladder((0,), inner, factors, [kept_pair_0], [], None, loads=True)
    kept_2, swapped_1, total = after((kept_2, swapped_1, total))
    kept_3 = z_swap(kept_2, 1)
    kept_pair_2 = x_gather(kept_2)
    swapped_pair_1 = x_gather(swapped_1)
    total = ladder((1, 0), inner, factors, [kept_pair_1], [swapped_pair_0], total)
    swapped_2, kept_3, total = after((swapped_2, kept_3, total))
    swapped_3 = z_swap(swapped_2, 1)
    swapped_pair_2 = x_gather(swapped_2)
    kept_pair_3 = (kept_3, z_swap(kept_pair_2[1], 1)) if inner == 2 else x_gather(kept_3)
    total = ladder((2, 1), inner, factors, [kept_pair_2], [swapped_pair_1], total)
    swapped_3, total = after((swapped_3, total))
    swapped_pair_3 = x_gather(swapped_3)
    total = ladder((3, 2), inner, factors, [kept_pair_3], [swapped_pair_2], total)

    middle = size // 2
    if inner == 2:
        sent_x, sent_z, own_x, own_z = ladder((3,), inner, factors, [], [swapped_pair_3], total, True)
        left = halved(own_x.reshape(2, 2, row_count, middle), x_swap(sent_x), z_low, lambda b: z_swap(b, 1))
        right = halved(own_z.reshape(2, 2, row_count, middle), z_swap(sent_z, 1), x_index, x_swap)
    else:
        total = ladder((3,), inner, factors, [], [swapped_pair_3], total)
        left = x_scatter(total[:, :middle].reshape(4, inner, row_count, middle))
        left = z_scatter(left.reshape(2, 2, row_count, middle), 1, 1, z_low)
        right = z_scatter(total[:, middle:].reshape(2, 2, GROUP_ROWS, middle), 1, 1, z_low)
        right = x_scatter(right.reshape(2, inner, row_count, middle))
    own_rows = jnp.concatenate([z_scatter(left, 0, 2, z_high), z_scatter(right, 0, 2, z_high)], axis=1)

    packed = own_rows.astype(jnp.bfloat16).reshape(row_count, vir_devices, row_count)
    packed = jnp.transpose(packed, (1, 2, 0))
    if inner == 2:
        def flipped(blocks):
            blocks = blocks.reshape(2, 2, *blocks.shape[1:])
            blocks = jnp.where(z_high == 1, jnp.flip(blocks, 0), blocks)
            blocks = jnp.where(z_low == 1, jnp.flip(blocks, 1), blocks)
            return blocks.reshape(4, *blocks.shape[2:])

        packed = packed.reshape(4, 2, row_count, row_count)
        stays = lax.dynamic_index_in_dim(packed, x_index, 1, keepdims=False)
        leaves = lax.dynamic_index_in_dim(packed, 1 - x_index, 1, keepdims=False)
        came = x_swap(leaves)
        first = jnp.where(x_index == 0, stays, came)
        second = jnp.where(x_index == 0, came, stays)
        turned = flipped(jnp.concatenate([first, second], axis=2))
        came = []
        for step in range(4):
            route = [
                (o * vir_devices + i, ((o + across) % occ_devices) * vir_devices + (i ^ 2 * step))
                for o in range(occ_devices)
                for i in range(vir_devices)
            ]
            came.append(lax.ppermute(turned[step], ("occ", "vir"), route))
        partner = flipped(jnp.stack(came))
    else:
        partner = y_swap(lax.all_to_all(packed, "vir", 0, 0))
    partner = jnp.transpose(partner, (1, 0, 2)).reshape(row_count, size).astype(jnp.float32)

    first = jnp.where(side == 0, own_rows, partner)
    second = jnp.where(side == 0, partner, own_rows)
    numerator = jnp.stack([first, second])

    pair_ids = lax.dynamic_slice_in_dim(pair_orbitals, occ_index * local_pairs, local_pairs, 0)
    row_start = vir_index * row_count
    energy_rows = lax.dynamic_slice_in_dim(vir_energy, row_start, row_count, 0)
    irrep_rows = lax.dynamic_slice_in_dim(vir_irrep, row_start, row_count, 0)
    positions = jnp.arange(occ_total, dtype=jnp.int32)
    first_hot = positions[None, :] == pair_ids[:, 0:1]
    second_hot = positions[None, :] == pair_ids[:, 1:2]
    pair_energy = jnp.sum(jnp.where(first_hot, occ_energy[None, :], 0.0), axis=1) + jnp.sum(
        jnp.where(second_hot, occ_energy[None, :], 0.0), axis=1
    )
    first_irrep = jnp.sum(jnp.where(first_hot, occ_irrep[None, :], 0), axis=1)
    second_irrep = jnp.sum(jnp.where(second_hot, occ_irrep[None, :], 0), axis=1)
    pair_sym = jnp.bitwise_xor(first_irrep, second_irrep)
    combined = jnp.bitwise_xor(
        jnp.bitwise_xor(pair_sym[:, None, None], irrep_rows[None, :, None]),
        vir_irrep[None, None, :],
    )
    allowed = combined == 0
    denominator = (
        energy_rows[None, :, None] + vir_energy[None, None, :] - pair_energy[:, None, None]
    )
    return jnp.where(allowed, numerator / denominator, jnp.float32(0.0))


def solution(mesh):
    return jax.shard_map(
        per_device,
        mesh=mesh,
        in_specs=(P("occ", "vir", None), P("vir", None, None), P(), P(), P(), P(), P()),
        out_specs=P("occ", "vir", None),
        check_vma=False,
    )
```

```python
import functools

import jax
import jax.numpy as jnp
from jax import lax
from jax.experimental import pallas as pl
from jax.experimental.pallas import tpu as pltpu
from jax.sharding import PartitionSpec as P

GROUP_ROWS = 256
VMEM_MIB = 16


def dot_nt(left, right):
    return lax.dot_general(left, right, (((1,), (1,)), ((), ())), preferred_element_type=jnp.float32)


def ladder_kernel(distances, kept_count, has_sums, loads, factor_ref, *refs):
    block_count = len(distances)
    vir_index = lax.axis_index("vir")
    z_index = vir_index // 2
    x_index = vir_index % 2
    z_low = z_index % 2
    pair_refs, refs = refs[: 2 * block_count], refs[2 * block_count :]
    before_refs = ()
    if has_sums:
        before_refs, refs = refs[:2], refs[2:]
    sent_x_ref, sent_z_ref, keep_x_ref, keep_z_ref, right_ref = refs[:5]
    refs = refs[5:]
    loading = []
    if loads:
        source_ref, factor_ref, factor_sem, refs = factor_ref, refs[0], refs[4], refs[1:4]
        for q in range(factor_ref.shape[0]):
            loading.append(pltpu.make_async_copy(source_ref.at[q], factor_ref.at[q], factor_sem.at[q]))
            loading[q].start()
    rows_ref, left_x_ref, left_z_ref = refs
    factor_count, size, _ = factor_ref.shape
    half = pair_refs[0].shape[0]
    width = block_count * GROUP_ROWS
    middle = size // 2

    for block in range(block_count):
        first = block * GROUP_ROWS + x_index * half
        second = block * GROUP_ROWS + (1 - x_index) * half
        rows_ref[pl.ds(pl.multiple_of(first, half), half), :] = pair_refs[2 * block][...]
        rows_ref[pl.ds(pl.multiple_of(second, half), half), :] = pair_refs[2 * block + 1][...]

    for q in range(factor_count):
        if loads:
            loading[q].wait()
        if block_count == 1:
            halves = dot_nt(rows_ref[...], factor_ref[q]).T.astype(jnp.bfloat16)
        else:
            halves = dot_nt(factor_ref[q], rows_ref[...]).astype(jnp.bfloat16)
        for block in range(block_count):
            column = pl.multiple_of((z_index ^ distances[block]) * GROUP_ROWS, GROUP_ROWS)
            taken = factor_ref[q, :, pl.ds(column, GROUP_ROWS)]
            made = halves[:, block * GROUP_ROWS : (block + 1) * GROUP_ROWS]
            target = pl.ds(q * width + block * GROUP_ROWS, GROUP_ROWS)
            left, right = (taken, made) if block < kept_count else (made, taken)
            right_ref[:, target] = right
            for start in range(0, size, 2 * half):
                low, high = left[start : start + half], left[start + half : start + 2 * half]
                here = pl.ds(start // 2, half)
                left_x_ref[here, target] = jnp.where(x_index == 0, high, low)
                keep_x_ref[here, target] = jnp.where(x_index == 0, low, high)
            for start in range(0, size, 2 * GROUP_ROWS):
                low = left[start : start + GROUP_ROWS]
                high = left[start + GROUP_ROWS : start + 2 * GROUP_ROWS]
                here = pl.ds(start // 2, GROUP_ROWS)
                left_z_ref[here, target] = jnp.where(z_low == 0, high, low)
                keep_z_ref[here, target] = jnp.where(z_low == 0, low, high)

    for number, (left_ref, out_ref) in enumerate(((left_x_ref, sent_x_ref), (left_z_ref, sent_z_ref))):
        product = dot_nt(left_ref[...], right_ref[pl.ds(number * middle, middle), :])
        if has_sums:
            product = product + before_refs[number][...]
        out_ref[...] = product.astype(out_ref.dtype)


def ladder(distances, factors, kept, swapped, sums=None, loads=False, last=False):
    factor_count, size, _ = factors.shape
    pairs = list(kept) + list(swapped)
    width = len(pairs) * GROUP_ROWS
    depth = factor_count * width
    middle = size // 2
    whole = pl.BlockSpec(memory_space=pltpu.VMEM)
    operands = [factors] + [half_block for pair in pairs for half_block in pair]
    aliases = {}
    if sums is not None:
        if not last:
            aliases = {len(operands): 0, len(operands) + 1: 1}
        operands += list(sums)
    in_specs = [whole] * len(operands)
    kind = jnp.bfloat16 if last else jnp.float32
    out_shape = [jax.ShapeDtypeStruct((middle, middle), kind)] * 2
    out_shape += [jax.ShapeDtypeStruct((rows, depth), jnp.bfloat16) for rows in (middle, middle, size)]
    scratch = [
        pltpu.VMEM((width, size), jnp.bfloat16),
        pltpu.VMEM((middle, depth), jnp.bfloat16),
        pltpu.VMEM((middle, depth), jnp.bfloat16),
    ]
    if loads:
        operands[0] = pltpu.with_memory_space_constraint(factors, pltpu.HBM)
        in_specs[0] = pl.BlockSpec(memory_space=pl.ANY)
        out_shape.append(jax.ShapeDtypeStruct(factors.shape, factors.dtype))
        scratch.append(pltpu.SemaphoreType.DMA((factor_count,)))
    out = pl.pallas_call(
        functools.partial(ladder_kernel, distances, len(kept), sums is not None, loads),
        out_shape=out_shape,
        in_specs=in_specs,
        out_specs=[whole] * len(out_shape),
        scratch_shapes=scratch,
        input_output_aliases=aliases,
        compiler_params=pltpu.CompilerParams(vmem_limit_bytes=VMEM_MIB * 1024 * 1024),
        cost_estimate=pl.CostEstimate(
            flops=(0 if loads else 3) * factor_count * width * size * size,
            bytes_accessed=2 * factor_count * size * size + 4 * size * size + 2 * width * size,
            transcendentals=0,
        ),
    )(*operands)
    return out[:2], tuple(out[2:5]), out[5:]


def keep_kernel(count, *refs):
    factors_refs, out_refs = refs[: 3 * count], refs[3 * count :]
    middle = out_refs[0].shape[0]
    for number, out_ref in enumerate(out_refs):
        total = None
        for part in range(count):
            left_ref, right_ref = factors_refs[3 * part + number], factors_refs[3 * part + 2]
            product = dot_nt(left_ref[...], right_ref[pl.ds(number * middle, middle), :])
            total = product if total is None else total + product
        out_ref[...] = total


def keep_sums(parts):
    middle = parts[0][0].shape[0]
    operands = [array for part in parts for array in part]
    whole = pl.BlockSpec(memory_space=pltpu.VMEM)
    return pl.pallas_call(
        functools.partial(keep_kernel, len(parts)),
        out_shape=[jax.ShapeDtypeStruct((middle, middle), jnp.float32)] * 2,
        in_specs=[whole] * len(operands),
        out_specs=[whole] * 2,
        compiler_params=pltpu.CompilerParams(vmem_limit_bytes=VMEM_MIB * 1024 * 1024),
        cost_estimate=pl.CostEstimate(
            flops=4 * middle * middle * sum(part[0].shape[1] for part in parts),
            bytes_accessed=2 * sum(array.size for array in operands) + 8 * middle * middle,
            transcendentals=0,
        ),
    )(*operands)


def per_device(amplitudes, factors, occ_energy, vir_energy, occ_irrep, vir_irrep, pair_orbitals):
    local_pairs, row_count, size = amplitudes.shape
    occ_total = occ_energy.shape[0]
    occ_devices = lax.axis_size("occ")
    vir_devices = lax.axis_size("vir")
    inner = GROUP_ROWS // row_count
    outer = vir_devices // inner
    assert local_pairs == 2 and outer == 4 and inner * row_count == GROUP_ROWS
    occ_index = lax.axis_index("occ")
    vir_index = lax.axis_index("vir")
    z_index = vir_index // inner
    x_index = vir_index % inner
    side = occ_index // (occ_devices // 2)
    across = occ_devices // 2

    def z_swap(block, distance):
        route = [(i, (i // inner ^ distance) * inner + i % inner) for i in range(vir_devices)]
        return lax.ppermute(block, "vir", route)

    def y_swap(block):
        return lax.ppermute(block, "occ", [(i, (i + across) % occ_devices) for i in range(occ_devices)])

    inner_groups = [[g * inner + i for i in range(inner)] for g in range(outer)]

    def x_swap(block):
        return lax.ppermute(block, "vir", [(i, i ^ 1) for i in range(vir_devices)])

    def x_pair(block):
        return block, x_swap(block)

    def x_scatter(sums):
        return lax.psum_scatter(sums, "vir", scatter_dimension=1, axis_index_groups=inner_groups)

    def z_scatter(sums, axis, distance, bit):
        sent = lax.dynamic_index_in_dim(sums, 1 - bit, axis, keepdims=False).astype(jnp.bfloat16)
        own = lax.dynamic_index_in_dim(sums, bit, axis, keepdims=False)
        return own + z_swap(sent, distance).astype(jnp.float32)

    def halved(own, came, bit, swap):
        came = came.reshape(own.shape)

        def half(index):
            mine = lax.dynamic_index_in_dim(own, index, 1, keepdims=False)
            theirs = lax.dynamic_index_in_dim(came, index, 1, keepdims=False)
            return mine + theirs.astype(jnp.float32)

        return half(bit) + swap(half(1 - bit).astype(jnp.bfloat16)).astype(jnp.float32)

    z_high = z_index // 2
    z_low = z_index % 2

    kept_0 = lax.dynamic_index_in_dim(amplitudes, side, 0, keepdims=False)
    given = lax.dynamic_index_in_dim(amplitudes, 1 - side, 0, keepdims=False)
    swapped_0 = y_swap(given)
    def step(distance, kept, swapped, total):
        return ladder((distance,), inner, factors, kept, swapped, total)

    after = lax.optimization_barrier
    middle = size // 2
    if inner == 2:
        kept_2 = z_swap(kept_0, 2)
        kept_1 = z_swap(kept_0, 1)
        kept_pair_0 = x_pair(kept_0)
        swapped_2 = z_swap(swapped_0, 2)
        swapped_1 = z_swap(swapped_0, 1)
        swapped_pair_0 = x_pair(swapped_0)
        kept_pair_1 = x_pair(kept_1)
        sums, part_0, (factors,) = ladder((0,), factors, [kept_pair_0], [], loads=True)
        kept_2, swapped_1, sums = after((kept_2, swapped_1, sums))
        kept_3 = z_swap(kept_2, 1)
        kept_pair_2 = x_pair(kept_2)
        swapped_pair_1 = x_pair(swapped_1)
        sums, part_1, _ = ladder((1, 0), factors, [kept_pair_1], [swapped_pair_0], sums)
        swapped_2, kept_3, sums = after((swapped_2, kept_3, sums))
        swapped_3 = z_swap(swapped_2, 1)
        swapped_pair_2 = x_pair(swapped_2)
        kept_pair_3 = (kept_3, z_swap(kept_pair_2[1], 1))
        sums, part_2, _ = ladder((2, 1), factors, [kept_pair_2], [swapped_pair_1], sums)
        swapped_3, sums = after((swapped_3, sums))
        swapped_pair_3 = x_pair(swapped_3)
        sums, part_3, _ = ladder((3, 2), factors, [kept_pair_3], [swapped_pair_2], sums)
        sent, part_4, _ = ladder((3,), factors, [], [swapped_pair_3], sums, last=True)
        own_x, own_z = keep_sums([part_0, part_1, part_2, part_3, part_4])
        shape = (2, 2, row_count, middle)
        left = halved(own_x.reshape(shape), x_swap(sent[0]), z_low, lambda b: z_swap(b, 1))
        right = halved(own_z.reshape(shape), z_swap(sent[1], 1), x_index, x_swap)
    else:
        kept_all = lax.all_gather(kept_0, "vir", axis=0, tiled=True)
        swapped_all = lax.all_gather(swapped_0, "vir", axis=0, tiled=True)
        kept_halves = jnp.einsum("cd,qbd->qcb", kept_all, factors, preferred_element_type=jnp.float32)
        swapped_halves = jnp.einsum("cd,qad->qca", swapped_all, factors, preferred_element_type=jnp.float32)
        total = jnp.einsum(
            "qac,qcb->ab", factors, kept_halves.astype(jnp.bfloat16), preferred_element_type=jnp.float32
        ) + jnp.einsum(
            "qca,qbc->ab", swapped_halves.astype(jnp.bfloat16), factors, preferred_element_type=jnp.float32
        )
        left = x_scatter(total[:, :middle].reshape(4, inner, row_count, middle))
        left = z_scatter(left.reshape(2, 2, row_count, middle), 1, 1, z_low)
        right = z_scatter(total[:, middle:].reshape(2, 2, GROUP_ROWS, middle), 1, 1, z_low)
        right = x_scatter(right.reshape(2, inner, row_count, middle))
    own_rows = jnp.concatenate([z_scatter(left, 0, 2, z_high), z_scatter(right, 0, 2, z_high)], axis=1)

    packed = own_rows.astype(jnp.bfloat16).reshape(row_count, vir_devices, row_count)
    packed = jnp.transpose(packed, (1, 2, 0))
    if inner == 2:
        def flipped(blocks):
            blocks = blocks.reshape(2, 2, *blocks.shape[1:])
            blocks = jnp.where(z_high == 1, jnp.flip(blocks, 0), blocks)
            blocks = jnp.where(z_low == 1, jnp.flip(blocks, 1), blocks)
            return blocks.reshape(4, *blocks.shape[2:])

        packed = packed.reshape(4, 2, row_count, row_count)
        stays = lax.dynamic_index_in_dim(packed, x_index, 1, keepdims=False)
        leaves = lax.dynamic_index_in_dim(packed, 1 - x_index, 1, keepdims=False)
        came = x_swap(leaves)
        first = jnp.where(x_index == 0, stays, came)
        second = jnp.where(x_index == 0, came, stays)
        turned = flipped(jnp.concatenate([first, second], axis=2))
        came = []
        for step in range(4):
            route = [
                (o * vir_devices + i, ((o + across) % occ_devices) * vir_devices + (i ^ 2 * step))
                for o in range(occ_devices)
                for i in range(vir_devices)
            ]
            came.append(lax.ppermute(turned[step], ("occ", "vir"), route))
        partner = flipped(jnp.stack(came))
    else:
        partner = y_swap(lax.all_to_all(packed, "vir", 0, 0))
    partner = jnp.transpose(partner, (1, 0, 2)).reshape(row_count, size).astype(jnp.float32)

    first = jnp.where(side == 0, own_rows, partner)
    second = jnp.where(side == 0, partner, own_rows)
    numerator = jnp.stack([first, second])

    pair_ids = lax.dynamic_slice_in_dim(pair_orbitals, occ_index * local_pairs, local_pairs, 0)
    row_start = vir_index * row_count
    energy_rows = lax.dynamic_slice_in_dim(vir_energy, row_start, row_count, 0)
    irrep_rows = lax.dynamic_slice_in_dim(vir_irrep, row_start, row_count, 0)
    positions = jnp.arange(occ_total, dtype=jnp.int32)
    first_hot = positions[None, :] == pair_ids[:, 0:1]
    second_hot = positions[None, :] == pair_ids[:, 1:2]
    pair_energy = jnp.sum(jnp.where(first_hot, occ_energy[None, :], 0.0), axis=1) + jnp.sum(
        jnp.where(second_hot, occ_energy[None, :], 0.0), axis=1
    )
    first_irrep = jnp.sum(jnp.where(first_hot, occ_irrep[None, :], 0), axis=1)
    second_irrep = jnp.sum(jnp.where(second_hot, occ_irrep[None, :], 0), axis=1)
    pair_sym = jnp.bitwise_xor(first_irrep, second_irrep)
    combined = jnp.bitwise_xor(
        jnp.bitwise_xor(pair_sym[:, None, None], irrep_rows[None, :, None]),
        vir_irrep[None, None, :],
    )
    allowed = combined == 0
    denominator = (
        energy_rows[None, :, None] + vir_energy[None, None, :] - pair_energy[:, None, None]
    )
    return jnp.where(allowed, numerator / denominator, jnp.float32(0.0))


def solution(mesh):
    return jax.shard_map(
        per_device,
        mesh=mesh,
        in_specs=(P("occ", "vir", None), P("vir", None, None), P(), P(), P(), P(), P()),
        out_specs=P("occ", "vir", None),
        check_vma=False,
    )
```

```python
import functools

import jax
import jax.numpy as jnp
from jax import lax
from jax.experimental import pallas as pl
from jax.experimental.pallas import tpu as pltpu
from jax.sharding import PartitionSpec as P

GROUP_ROWS = 256
VMEM_MIB = 8


def dot_nt(left, right):
    return lax.dot_general(left, right, (((1,), (1,)), ((), ())), preferred_element_type=jnp.float32)


def ladder_kernel(distances, kept_count, has_sums, loads, factor_ref, *refs):
    block_count = len(distances)
    vir_index = lax.axis_index("vir")
    z_index = vir_index // 2
    x_index = vir_index % 2
    z_low = z_index % 2
    pair_refs, refs = refs[: 2 * block_count], refs[2 * block_count :]
    before_refs = ()
    if has_sums:
        before_refs, refs = refs[:2], refs[2:]
    sent_x_ref, sent_z_ref, left_ref, right_ref = refs[:4]
    refs = refs[4:]
    loading = []
    if loads:
        source_ref, factor_ref, factor_sem, refs = factor_ref, refs[0], refs[2], refs[1:2]
        for q in range(factor_ref.shape[0]):
            loading.append(pltpu.make_async_copy(source_ref.at[q], factor_ref.at[q], factor_sem.at[q]))
            loading[q].start()
    (rows_ref,) = refs
    factor_count, size, _ = factor_ref.shape
    half = pair_refs[0].shape[0]
    width = block_count * GROUP_ROWS
    middle = size // 2

    for block in range(block_count):
        first = block * GROUP_ROWS + x_index * half
        second = block * GROUP_ROWS + (1 - x_index) * half
        rows_ref[pl.ds(pl.multiple_of(first, half), half), :] = pair_refs[2 * block][...]
        rows_ref[pl.ds(pl.multiple_of(second, half), half), :] = pair_refs[2 * block + 1][...]

    for q in range(factor_count):
        if loads:
            loading[q].wait()
        if block_count == 1:
            halves = dot_nt(rows_ref[...], factor_ref[q]).T.astype(jnp.bfloat16)
        else:
            halves = dot_nt(factor_ref[q], rows_ref[...]).astype(jnp.bfloat16)
        for block in range(block_count):
            column = pl.multiple_of((z_index ^ distances[block]) * GROUP_ROWS, GROUP_ROWS)
            taken = factor_ref[q, :, pl.ds(column, GROUP_ROWS)]
            made = halves[:, block * GROUP_ROWS : (block + 1) * GROUP_ROWS]
            target = pl.ds(q * width + block * GROUP_ROWS, GROUP_ROWS)
            left, right = (taken, made) if block < kept_count else (made, taken)
            for start in range(0, size, 2 * half):
                low, high = right[start : start + half], right[start + half : start + 2 * half]
                first = start // middle * middle + start % middle // 2
                right_ref[pl.ds(first, half), target] = jnp.where(x_index == 0, low, high)
                right_ref[pl.ds(first + GROUP_ROWS, half), target] = jnp.where(x_index == 0, high, low)
            for start in range(0, size, 2 * GROUP_ROWS):
                low = left[start : start + GROUP_ROWS]
                high = left[start + GROUP_ROWS : start + 2 * GROUP_ROWS]
                left_ref[pl.ds(start // 2, GROUP_ROWS), target] = jnp.where(z_low == 0, low, high)
                left_ref[pl.ds(middle + start // 2, GROUP_ROWS), target] = jnp.where(z_low == 0, high, low)

    products = (
        dot_nt(right_ref[pl.ds(GROUP_ROWS, GROUP_ROWS), :], left_ref[...]),
        dot_nt(right_ref[pl.ds(middle, middle), :], left_ref[pl.ds(middle, middle), :]),
    )
    for number, out_ref in enumerate((sent_x_ref, sent_z_ref)):
        product = products[number]
        if has_sums:
            product = product + before_refs[number][...]
        out_ref[...] = product.astype(out_ref.dtype)


def ladder(distances, factors, kept, swapped, sums=None, loads=False, last=False):
    factor_count, size, _ = factors.shape
    pairs = list(kept) + list(swapped)
    width = len(pairs) * GROUP_ROWS
    depth = factor_count * width
    middle = size // 2
    whole = pl.BlockSpec(memory_space=pltpu.VMEM)
    operands = [factors] + [half_block for pair in pairs for half_block in pair]
    aliases = {}
    if sums is not None:
        if not last:
            aliases = {len(operands): 0, len(operands) + 1: 1}
        operands += list(sums)
    in_specs = [whole] * len(operands)
    kind = jnp.bfloat16 if last else jnp.float32
    out_shape = [jax.ShapeDtypeStruct(shape, kind) for shape in ((GROUP_ROWS, size), (middle, middle))]
    out_shape += [jax.ShapeDtypeStruct((size, depth), jnp.bfloat16)] * 2
    scratch = [
        pltpu.VMEM((width, size), jnp.bfloat16),
    ]
    if loads:
        operands[0] = pltpu.with_memory_space_constraint(factors, pltpu.HBM)
        in_specs[0] = pl.BlockSpec(memory_space=pl.ANY)
        out_shape.append(jax.ShapeDtypeStruct(factors.shape, factors.dtype))
        scratch.append(pltpu.SemaphoreType.DMA((factor_count,)))
    out = pl.pallas_call(
        functools.partial(ladder_kernel, distances, len(kept), sums is not None, loads),
        out_shape=out_shape,
        in_specs=in_specs,
        out_specs=[whole] * len(out_shape),
        scratch_shapes=scratch,
        input_output_aliases=aliases,
        compiler_params=pltpu.CompilerParams(vmem_limit_bytes=VMEM_MIB * 1024 * 1024),
        cost_estimate=pl.CostEstimate(
            flops=(0 if loads else 2) * factor_count * width * size * size,
            bytes_accessed=2 * factor_count * size * size + 4 * size * size + 2 * width * size,
            transcendentals=0,
        ),
    )(*operands)
    return out[:2], tuple(out[2:4]), out[4:]


def keep_kernel(count, *refs):
    parts, (keep_x_ref, keep_z_ref) = refs[: 2 * count], refs[2 * count :]
    middle = keep_z_ref.shape[0]
    totals = [None, None]
    for part in range(count):
        left_ref, right_ref = parts[2 * part], parts[2 * part + 1]
        products = (
            dot_nt(right_ref[pl.ds(0, GROUP_ROWS), :], left_ref[...]),
            dot_nt(right_ref[pl.ds(middle, middle), :], left_ref[pl.ds(0, middle), :]),
        )
        totals = [p if t is None else t + p for t, p in zip(totals, products)]
    keep_x_ref[...] = totals[0]
    keep_z_ref[...] = totals[1]


def keep_sums(parts):
    size = parts[0][0].shape[0]
    middle = size // 2
    operands = [array for part in parts for array in part]
    whole = pl.BlockSpec(memory_space=pltpu.VMEM)
    return pl.pallas_call(
        functools.partial(keep_kernel, len(parts)),
        out_shape=[jax.ShapeDtypeStruct(shape, jnp.float32) for shape in ((GROUP_ROWS, size), (middle, middle))],
        in_specs=[whole] * len(operands),
        out_specs=[whole] * 2,
        compiler_params=pltpu.CompilerParams(vmem_limit_bytes=VMEM_MIB * 1024 * 1024),
        cost_estimate=pl.CostEstimate(
            flops=4 * middle * middle * sum(part[0].shape[1] for part in parts),
            bytes_accessed=2 * sum(array.size for array in operands) + 8 * middle * middle,
            transcendentals=0,
        ),
    )(*operands)


def per_device(amplitudes, factors, occ_energy, vir_energy, occ_irrep, vir_irrep, pair_orbitals):
    local_pairs, row_count, size = amplitudes.shape
    occ_total = occ_energy.shape[0]
    occ_devices = lax.axis_size("occ")
    vir_devices = lax.axis_size("vir")
    inner = GROUP_ROWS // row_count
    outer = vir_devices // inner
    assert local_pairs == 2 and outer == 4 and inner * row_count == GROUP_ROWS
    occ_index = lax.axis_index("occ")
    vir_index = lax.axis_index("vir")
    z_index = vir_index // inner
    x_index = vir_index % inner
    side = occ_index // (occ_devices // 2)
    across = occ_devices // 2

    def z_swap(block, distance):
        route = [(i, (i // inner ^ distance) * inner + i % inner) for i in range(vir_devices)]
        return lax.ppermute(block, "vir", route)

    def y_swap(block):
        return lax.ppermute(block, "occ", [(i, (i + across) % occ_devices) for i in range(occ_devices)])

    inner_groups = [[g * inner + i for i in range(inner)] for g in range(outer)]

    def x_swap(block):
        return lax.ppermute(block, "vir", [(i, i ^ 1) for i in range(vir_devices)])

    def x_pair(block):
        return block, x_swap(block)

    def x_scatter(sums):
        return lax.psum_scatter(sums, "vir", scatter_dimension=1, axis_index_groups=inner_groups)

    def z_scatter(sums, axis, distance, bit):
        sent = lax.dynamic_index_in_dim(sums, 1 - bit, axis, keepdims=False).astype(jnp.bfloat16)
        own = lax.dynamic_index_in_dim(sums, bit, axis, keepdims=False)
        return own + z_swap(sent, distance).astype(jnp.float32)

    z_high = z_index // 2
    z_low = z_index % 2

    kept_0 = lax.dynamic_index_in_dim(amplitudes, side, 0, keepdims=False)
    given = lax.dynamic_index_in_dim(amplitudes, 1 - side, 0, keepdims=False)
    swapped_0 = y_swap(given)
    def step(distance, kept, swapped, total):
        return ladder((distance,), inner, factors, kept, swapped, total)

    after = lax.optimization_barrier
    def gated(block, part):
        return after((block, part[0]))[0]

    middle = size // 2
    if inner == 2:
        kept_1 = z_swap(kept_0, 1)
        kept_pair_0 = x_pair(kept_0)
        kept_2 = z_swap(kept_0, 2)
        swapped_2 = z_swap(swapped_0, 2)
        swapped_1 = z_swap(swapped_0, 1)
        swapped_pair_0 = x_pair(swapped_0)
        kept_pair_1 = x_pair(kept_1)
        sums, part_0, (factors,) = ladder((0,), factors, [kept_pair_0], [], loads=True)
        kept_2, swapped_1, sums = after((kept_2, swapped_1, sums))
        kept_3 = z_swap(kept_2, 1)
        kept_pair_2 = x_pair(kept_2)
        swapped_pair_1 = x_pair(swapped_1)
        sums, part_1, _ = ladder((1, 0), factors, [kept_pair_1], [swapped_pair_0], sums)
        swapped_3 = z_swap(gated(swapped_2, part_0), 1)
        swapped_pair_2 = x_pair(gated(swapped_2, part_1))
        kept_pair_3 = (kept_3, z_swap(gated(kept_pair_2[1], part_1), 1))
        sums, part_2, _ = ladder((2, 1), factors, [kept_pair_2], [swapped_pair_1], sums)
        swapped_pair_3 = x_pair(gated(swapped_3, part_2))
        sums, part_3, _ = ladder((3, 2), factors, [kept_pair_3], [swapped_pair_2], sums)
        sent, part_4, _ = ladder((3,), factors, [], [swapped_pair_3], sums, last=True)
        keep_x, keep_z = keep_sums([part_0, part_1, part_2, part_3, part_4])
        came_x = x_swap(sent[0])
        came_z = z_swap(sent[1], 1)

        def added(own, came):
            return own + came.astype(jnp.float32)

        def high_half(block, index):
            return jnp.where(index == 0, block[:, :GROUP_ROWS], block[:, GROUP_ROWS:])

        first = added(keep_x[:, :middle], came_x[:, :middle])
        leaving = added(keep_x[:, middle:], came_x[:, middle:]).astype(jnp.bfloat16)
        left = added(first, z_swap(leaving, 1))
        first = added(keep_z[:GROUP_ROWS], came_z[:GROUP_ROWS])
        leaving = added(keep_z[GROUP_ROWS:], came_z[GROUP_ROWS:]).astype(jnp.bfloat16)
        right = added(first, x_swap(leaving))
        left = added(
            high_half(left, z_high), z_swap(high_half(left, 1 - z_high).astype(jnp.bfloat16), 2)
        )
        right = added(
            high_half(right, z_high), z_swap(high_half(right, 1 - z_high).astype(jnp.bfloat16), 2)
        )
        turned = jnp.concatenate([left, right], axis=0)
        own_half = jnp.where(x_index == 0, turned[:, :row_count], turned[:, row_count:])
        other_half = x_swap(jnp.where(x_index == 0, turned[:, row_count:], turned[:, :row_count]))
        by_x = jnp.stack(
            [jnp.where(x_index == 0, own_half, other_half), jnp.where(x_index == 0, other_half, own_half)]
        ).reshape(2, 4, row_count, row_count)
        own_rows = jnp.transpose(by_x, (3, 1, 0, 2)).reshape(row_count, size)
        turned = turned.astype(jnp.bfloat16).reshape(4, row_count, GROUP_ROWS)
    else:
        kept_all = lax.all_gather(kept_0, "vir", axis=0, tiled=True)
        swapped_all = lax.all_gather(swapped_0, "vir", axis=0, tiled=True)
        kept_halves = jnp.einsum("cd,qbd->qcb", kept_all, factors, preferred_element_type=jnp.float32)
        swapped_halves = jnp.einsum("cd,qad->qca", swapped_all, factors, preferred_element_type=jnp.float32)
        total = jnp.einsum(
            "qac,qcb->ab", factors, kept_halves.astype(jnp.bfloat16), preferred_element_type=jnp.float32
        ) + jnp.einsum(
            "qca,qbc->ab", swapped_halves.astype(jnp.bfloat16), factors, preferred_element_type=jnp.float32
        )
        left = x_scatter(total[:, :middle].reshape(4, inner, row_count, middle))
        left = z_scatter(left.reshape(2, 2, row_count, middle), 1, 1, z_low)
        right = z_scatter(total[:, middle:].reshape(2, 2, GROUP_ROWS, middle), 1, 1, z_low)
        right = x_scatter(right.reshape(2, inner, row_count, middle))
        own_rows = jnp.concatenate([z_scatter(left, 0, 2, z_high), z_scatter(right, 0, 2, z_high)], axis=1)
        packed = own_rows.astype(jnp.bfloat16).reshape(row_count, vir_devices, row_count)
        packed = jnp.transpose(packed, (1, 2, 0))
    if inner == 2:
        def flipped(blocks):
            blocks = blocks.reshape(2, 2, *blocks.shape[1:])
            blocks = jnp.where(z_high == 1, jnp.flip(blocks, 0), blocks)
            blocks = jnp.where(z_low == 1, jnp.flip(blocks, 1), blocks)
            return blocks.reshape(4, *blocks.shape[2:])

        turned = flipped(turned)
        came = []
        for step in range(4):
            route = [
                (o * vir_devices + i, ((o + across) % occ_devices) * vir_devices + (i ^ 2 * step))
                for o in range(occ_devices)
                for i in range(vir_devices)
            ]
            leaving = turned[step]
            if step == 3:
                leaving = after((leaving, other_half))[0]
            came.append(lax.ppermute(leaving, ("occ", "vir"), route))
        partner = flipped(jnp.stack(came))
    else:
        partner = y_swap(lax.all_to_all(packed, "vir", 0, 0))
    partner = jnp.transpose(partner, (1, 0, 2)).reshape(row_count, size).astype(jnp.float32)

    first = jnp.where(side == 0, own_rows, partner)
    second = jnp.where(side == 0, partner, own_rows)
    numerator = jnp.stack([first, second])

    if inner == 2:
        small = (occ_energy, vir_energy, occ_irrep, vir_irrep, pair_orbitals)
        small = after((*small, part_4[0]))[:5]
        occ_energy, vir_energy, occ_irrep, vir_irrep, pair_orbitals = small
    pair_ids = lax.dynamic_slice_in_dim(pair_orbitals, occ_index * local_pairs, local_pairs, 0)
    row_start = vir_index * row_count
    energy_rows = lax.dynamic_slice_in_dim(vir_energy, row_start, row_count, 0)
    irrep_rows = lax.dynamic_slice_in_dim(vir_irrep, row_start, row_count, 0)
    positions = jnp.arange(occ_total, dtype=jnp.int32)
    first_hot = positions[None, :] == pair_ids[:, 0:1]
    second_hot = positions[None, :] == pair_ids[:, 1:2]
    pair_energy = jnp.sum(jnp.where(first_hot, occ_energy[None, :], 0.0), axis=1) + jnp.sum(
        jnp.where(second_hot, occ_energy[None, :], 0.0), axis=1
    )
    first_irrep = jnp.sum(jnp.where(first_hot, occ_irrep[None, :], 0), axis=1)
    second_irrep = jnp.sum(jnp.where(second_hot, occ_irrep[None, :], 0), axis=1)
    pair_sym = jnp.bitwise_xor(first_irrep, second_irrep)
    combined = jnp.bitwise_xor(
        jnp.bitwise_xor(pair_sym[:, None, None], irrep_rows[None, :, None]),
        vir_irrep[None, None, :],
    )
    allowed = combined == 0
    denominator = (
        energy_rows[None, :, None] + vir_energy[None, None, :] - pair_energy[:, None, None]
    )
    return jnp.where(allowed, numerator / denominator, jnp.float32(0.0))


def solution(mesh):
    return jax.shard_map(
        per_device,
        mesh=mesh,
        in_specs=(P("occ", "vir", None), P("vir", None, None), P(), P(), P(), P(), P()),
        out_specs=P("occ", "vir", None),
        check_vma=False,
    )
```

```python
import functools

import jax
import jax.numpy as jnp
from jax import lax
from jax.experimental import pallas as pl
from jax.experimental.pallas import tpu as pltpu
from jax.sharding import PartitionSpec as P

GROUP_ROWS = 256
VMEM_MIB = 8


def dot_nt(left, right):
    return lax.dot_general(left, right, (((1,), (1,)), ((), ())), preferred_element_type=jnp.float32)


def ladder_kernel(distances, kept_count, has_sums, loads, factor_ref, *refs):
    block_count = len(distances)
    vir_index = lax.axis_index("vir")
    z_index = vir_index // 2
    x_index = vir_index % 2
    z_low = z_index % 2
    pair_refs, refs = refs[: 2 * block_count], refs[2 * block_count :]
    before_refs = ()
    if has_sums:
        before_refs, refs = refs[:2], refs[2:]
    sent_x_ref, sent_z_ref, left_ref, right_ref = refs[:4]
    refs = refs[4:]
    loading = []
    if loads:
        source_ref, factor_ref, factor_sem, refs = factor_ref, refs[0], refs[2], refs[1:2]
        for q in range(factor_ref.shape[0]):
            loading.append(pltpu.make_async_copy(source_ref.at[q], factor_ref.at[q], factor_sem.at[q]))
            loading[q].start()
    (rows_ref,) = refs
    factor_count, size, _ = factor_ref.shape
    half = pair_refs[0].shape[0]
    width = block_count * GROUP_ROWS
    middle = size // 2

    for block in range(block_count):
        first = block * GROUP_ROWS + x_index * half
        second = block * GROUP_ROWS + (1 - x_index) * half
        rows_ref[pl.ds(pl.multiple_of(first, half), half), :] = pair_refs[2 * block][...]
        rows_ref[pl.ds(pl.multiple_of(second, half), half), :] = pair_refs[2 * block + 1][...]

    for q in range(factor_count):
        if loads:
            loading[q].wait()
        if block_count == 1:
            halves = dot_nt(rows_ref[...], factor_ref[q]).T.astype(jnp.bfloat16)
        else:
            halves = dot_nt(factor_ref[q], rows_ref[...]).astype(jnp.bfloat16)
        for block in range(block_count):
            column = pl.multiple_of((z_index ^ distances[block]) * GROUP_ROWS, GROUP_ROWS)
            taken = factor_ref[q, :, pl.ds(column, GROUP_ROWS)]
            made = halves[:, block * GROUP_ROWS : (block + 1) * GROUP_ROWS]
            target = pl.ds(q * width + block * GROUP_ROWS, GROUP_ROWS)
            left, right = (taken, made) if block < kept_count else (made, taken)
            for start in range(0, size, 2 * half):
                low, high = right[start : start + half], right[start + half : start + 2 * half]
                first = start // middle * middle + start % middle // 2
                right_ref[pl.ds(first, half), target] = jnp.where(x_index == 0, low, high)
                right_ref[pl.ds(first + GROUP_ROWS, half), target] = jnp.where(x_index == 0, high, low)
            for start in range(0, size, 2 * GROUP_ROWS):
                low = left[start : start + GROUP_ROWS]
                high = left[start + GROUP_ROWS : start + 2 * GROUP_ROWS]
                left_ref[pl.ds(start // 2, GROUP_ROWS), target] = jnp.where(z_low == 0, low, high)
                left_ref[pl.ds(middle + start // 2, GROUP_ROWS), target] = jnp.where(z_low == 0, high, low)

    products = (
        dot_nt(right_ref[pl.ds(GROUP_ROWS, GROUP_ROWS), :], left_ref[...]),
        dot_nt(right_ref[pl.ds(middle, middle), :], left_ref[pl.ds(middle, middle), :]),
    )
    for number, out_ref in enumerate((sent_x_ref, sent_z_ref)):
        product = products[number]
        if has_sums:
            product = product + before_refs[number][...]
        out_ref[...] = product.astype(out_ref.dtype)


def ladder(distances, factors, kept, swapped, sums=None, loads=False, last=False):
    factor_count, size, _ = factors.shape
    pairs = list(kept) + list(swapped)
    width = len(pairs) * GROUP_ROWS
    depth = factor_count * width
    middle = size // 2
    whole = pl.BlockSpec(memory_space=pltpu.VMEM)
    operands = [factors] + [half_block for pair in pairs for half_block in pair]
    aliases = {}
    if sums is not None:
        if not last:
            aliases = {len(operands): 0, len(operands) + 1: 1}
        operands += list(sums)
    in_specs = [whole] * len(operands)
    kind = jnp.bfloat16 if last else jnp.float32
    out_shape = [jax.ShapeDtypeStruct(shape, kind) for shape in ((GROUP_ROWS, size), (middle, middle))]
    out_shape += [jax.ShapeDtypeStruct((size, depth), jnp.bfloat16)] * 2
    scratch = [
        pltpu.VMEM((width, size), jnp.bfloat16),
    ]
    if loads:
        operands[0] = pltpu.with_memory_space_constraint(factors, pltpu.HBM)
        in_specs[0] = pl.BlockSpec(memory_space=pl.ANY)
        out_shape.append(jax.ShapeDtypeStruct(factors.shape, factors.dtype))
        scratch.append(pltpu.SemaphoreType.DMA((factor_count,)))
    out = pl.pallas_call(
        functools.partial(ladder_kernel, distances, len(kept), sums is not None, loads),
        out_shape=out_shape,
        in_specs=in_specs,
        out_specs=[whole] * len(out_shape),
        scratch_shapes=scratch,
        input_output_aliases=aliases,
        compiler_params=pltpu.CompilerParams(vmem_limit_bytes=VMEM_MIB * 1024 * 1024),
        cost_estimate=pl.CostEstimate(
            flops=(1 if loads else 2) * factor_count * width * size * size,
            bytes_accessed=2 * factor_count * size * size + 4 * size * size + 2 * width * size,
            transcendentals=0,
        ),
    )(*operands)
    return out[:2], tuple(out[2:4]), out[4:]


def keep_kernel(count, *refs):
    parts, (keep_x_ref, keep_z_ref) = refs[: 2 * count], refs[2 * count :]
    middle = keep_z_ref.shape[0]
    totals = [None, None]
    for part in range(count):
        left_ref, right_ref = parts[2 * part], parts[2 * part + 1]
        products = (
            dot_nt(right_ref[pl.ds(0, GROUP_ROWS), :], left_ref[...]),
            dot_nt(right_ref[pl.ds(middle, middle), :], left_ref[pl.ds(0, middle), :]),
        )
        totals = [p if t is None else t + p for t, p in zip(totals, products)]
    keep_x_ref[...] = totals[0]
    keep_z_ref[...] = totals[1]


def keep_sums(parts):
    size = parts[0][0].shape[0]
    middle = size // 2
    operands = [array for part in parts for array in part]
    whole = pl.BlockSpec(memory_space=pltpu.VMEM)
    return pl.pallas_call(
        functools.partial(keep_kernel, len(parts)),
        out_shape=[jax.ShapeDtypeStruct(shape, jnp.float32) for shape in ((GROUP_ROWS, size), (middle, middle))],
        in_specs=[whole] * len(operands),
        out_specs=[whole] * 2,
        compiler_params=pltpu.CompilerParams(vmem_limit_bytes=VMEM_MIB * 1024 * 1024),
        cost_estimate=pl.CostEstimate(
            flops=4 * middle * middle * sum(part[0].shape[1] for part in parts),
            bytes_accessed=2 * sum(array.size for array in operands) + 8 * middle * middle,
            transcendentals=0,
        ),
    )(*operands)


def per_device(amplitudes, factors, occ_energy, vir_energy, occ_irrep, vir_irrep, pair_orbitals):
    local_pairs, row_count, size = amplitudes.shape
    occ_total = occ_energy.shape[0]
    occ_devices = lax.axis_size("occ")
    vir_devices = lax.axis_size("vir")
    inner = GROUP_ROWS // row_count
    outer = vir_devices // inner
    assert local_pairs == 2 and outer == 4 and inner * row_count == GROUP_ROWS
    occ_index = lax.axis_index("occ")
    vir_index = lax.axis_index("vir")
    z_index = vir_index // inner
    x_index = vir_index % inner
    side = occ_index // (occ_devices // 2)
    across = occ_devices // 2

    def z_swap(block, distance):
        route = [(i, (i // inner ^ distance) * inner + i % inner) for i in range(vir_devices)]
        return lax.ppermute(block, "vir", route)

    def y_swap(block):
        return lax.ppermute(block, "occ", [(i, (i + across) % occ_devices) for i in range(occ_devices)])

    inner_groups = [[g * inner + i for i in range(inner)] for g in range(outer)]

    def x_swap(block):
        return lax.ppermute(block, "vir", [(i, i ^ 1) for i in range(vir_devices)])

    def x_pair(block):
        return block, x_swap(block)

    def x_scatter(sums):
        return lax.psum_scatter(sums, "vir", scatter_dimension=1, axis_index_groups=inner_groups)

    def z_scatter(sums, axis, distance, bit):
        sent = lax.dynamic_index_in_dim(sums, 1 - bit, axis, keepdims=False).astype(jnp.bfloat16)
        own = lax.dynamic_index_in_dim(sums, bit, axis, keepdims=False)
        return own + z_swap(sent, distance).astype(jnp.float32)

    z_high = z_index // 2
    z_low = z_index % 2

    kept_0 = lax.dynamic_index_in_dim(amplitudes, side, 0, keepdims=False)
    given = lax.dynamic_index_in_dim(amplitudes, 1 - side, 0, keepdims=False)
    swapped_0 = y_swap(given)
    def step(distance, kept, swapped, total):
        return ladder((distance,), inner, factors, kept, swapped, total)

    after = lax.optimization_barrier
    def gated(block, part):
        return after((block, part[0]))[0]

    middle = size // 2
    if inner == 2:
        kept_1 = z_swap(kept_0, 1)
        kept_pair_0 = x_pair(kept_0)
        kept_2 = z_swap(kept_0, 2)
        swapped_2 = z_swap(swapped_0, 2)
        swapped_1 = z_swap(swapped_0, 1)
        swapped_pair_0 = x_pair(swapped_0)
        kept_pair_1 = x_pair(kept_1)
        sums, part_0, (factors,) = ladder((0,), factors, [kept_pair_0], [], loads=True)
        kept_2, swapped_1, sums = after((kept_2, swapped_1, sums))
        kept_3 = z_swap(kept_2, 1)
        kept_pair_2 = x_pair(kept_2)
        swapped_pair_1 = x_pair(swapped_1)
        sums, part_1, _ = ladder((1, 0), factors, [kept_pair_1], [swapped_pair_0], sums)
        swapped_3 = z_swap(gated(swapped_2, part_0), 1)
        swapped_pair_2 = x_pair(gated(swapped_2, part_1))
        kept_pair_3 = (kept_3, z_swap(gated(kept_pair_2[1], part_1), 1))
        sums, part_2, _ = ladder((2, 1), factors, [kept_pair_2], [swapped_pair_1], sums)
        swapped_pair_3 = x_pair(gated(swapped_3, part_2))
        sums, part_3, _ = ladder((3, 2), factors, [kept_pair_3], [swapped_pair_2], sums)
        sent, part_4, _ = ladder((3,), factors, [], [swapped_pair_3], sums, last=True)
        keep_x, keep_z = keep_sums([part_0, part_1, part_2, part_3, part_4])
        came_x = x_swap(sent[0])
        came_z = z_swap(sent[1], 1)

        def added(own, came):
            return own + came.astype(jnp.float32)

        def high_half(block, index):
            return jnp.where(index == 0, block[:, :GROUP_ROWS], block[:, GROUP_ROWS:])

        first = added(keep_x[:, :middle], came_x[:, :middle])
        leaving = added(keep_x[:, middle:], came_x[:, middle:]).astype(jnp.bfloat16)
        left = added(first, z_swap(leaving, 1))
        first = added(keep_z[:GROUP_ROWS], came_z[:GROUP_ROWS])
        leaving = added(keep_z[GROUP_ROWS:], came_z[GROUP_ROWS:]).astype(jnp.bfloat16)
        right = added(first, x_swap(leaving))
        left = added(
            high_half(left, z_high), z_swap(high_half(left, 1 - z_high).astype(jnp.bfloat16), 2)
        )
        right = added(
            high_half(right, z_high), z_swap(high_half(right, 1 - z_high).astype(jnp.bfloat16), 2)
        )
        turned = jnp.concatenate([left, right], axis=0)
        own_half = jnp.where(x_index == 0, turned[:, :row_count], turned[:, row_count:])
        other_half = jnp.concatenate(
            [
                x_swap(jnp.where(x_index == 0, part[:, row_count:], part[:, :row_count]))
                for part in (left, right)
            ],
            axis=0,
        )
        by_x = jnp.stack(
            [jnp.where(x_index == 0, own_half, other_half), jnp.where(x_index == 0, other_half, own_half)]
        ).reshape(2, 4, row_count, row_count)
        own_rows = jnp.transpose(by_x, (3, 1, 0, 2)).reshape(row_count, size)
        turned = turned.astype(jnp.bfloat16).reshape(4, row_count, GROUP_ROWS)
    else:
        kept_all = lax.all_gather(kept_0, "vir", axis=0, tiled=True)
        swapped_all = lax.all_gather(swapped_0, "vir", axis=0, tiled=True)
        kept_halves = jnp.einsum("cd,qbd->qcb", kept_all, factors, preferred_element_type=jnp.float32)
        swapped_halves = jnp.einsum("cd,qad->qca", swapped_all, factors, preferred_element_type=jnp.float32)
        total = jnp.einsum(
            "qac,qcb->ab", factors, kept_halves.astype(jnp.bfloat16), preferred_element_type=jnp.float32
        ) + jnp.einsum(
            "qca,qbc->ab", swapped_halves.astype(jnp.bfloat16), factors, preferred_element_type=jnp.float32
        )
        left = x_scatter(total[:, :middle].reshape(4, inner, row_count, middle))
        left = z_scatter(left.reshape(2, 2, row_count, middle), 1, 1, z_low)
        right = z_scatter(total[:, middle:].reshape(2, 2, GROUP_ROWS, middle), 1, 1, z_low)
        right = x_scatter(right.reshape(2, inner, row_count, middle))
        own_rows = jnp.concatenate([z_scatter(left, 0, 2, z_high), z_scatter(right, 0, 2, z_high)], axis=1)
        packed = own_rows.astype(jnp.bfloat16).reshape(row_count, vir_devices, row_count)
        packed = jnp.transpose(packed, (1, 2, 0))
    if inner == 2:
        def flipped(blocks):
            blocks = blocks.reshape(2, 2, *blocks.shape[1:])
            blocks = jnp.where(z_high == 1, jnp.flip(blocks, 0), blocks)
            blocks = jnp.where(z_low == 1, jnp.flip(blocks, 1), blocks)
            return blocks.reshape(4, *blocks.shape[2:])

        turned = flipped(turned)
        came = []
        for step in range(4):
            route = [
                (o * vir_devices + i, ((o + across) % occ_devices) * vir_devices + (i ^ 2 * step))
                for o in range(occ_devices)
                for i in range(vir_devices)
            ]
            leaving = turned[step]
            if step == 1:
                leaving = after((leaving, other_half))[0]
            came.append(lax.ppermute(leaving, ("occ", "vir"), route))
        partner = flipped(jnp.stack(came))
    else:
        partner = y_swap(lax.all_to_all(packed, "vir", 0, 0))
    partner = jnp.transpose(partner, (1, 0, 2)).reshape(row_count, size).astype(jnp.float32)

    first = jnp.where(side == 0, own_rows, partner)
    second = jnp.where(side == 0, partner, own_rows)
    numerator = jnp.stack([first, second])

    if inner == 2:
        small = (occ_energy, vir_energy, occ_irrep, vir_irrep, pair_orbitals)
        small = after((*small, part_4[0]))[:5]
        occ_energy, vir_energy, occ_irrep, vir_irrep, pair_orbitals = small
    pair_ids = lax.dynamic_slice_in_dim(pair_orbitals, occ_index * local_pairs, local_pairs, 0)
    row_start = vir_index * row_count
    energy_rows = lax.dynamic_slice_in_dim(vir_energy, row_start, row_count, 0)
    irrep_rows = lax.dynamic_slice_in_dim(vir_irrep, row_start, row_count, 0)
    positions = jnp.arange(occ_total, dtype=jnp.int32)
    first_hot = positions[None, :] == pair_ids[:, 0:1]
    second_hot = positions[None, :] == pair_ids[:, 1:2]
    pair_energy = jnp.sum(jnp.where(first_hot, occ_energy[None, :], 0.0), axis=1) + jnp.sum(
        jnp.where(second_hot, occ_energy[None, :], 0.0), axis=1
    )
    first_irrep = jnp.sum(jnp.where(first_hot, occ_irrep[None, :], 0), axis=1)
    second_irrep = jnp.sum(jnp.where(second_hot, occ_irrep[None, :], 0), axis=1)
    pair_sym = jnp.bitwise_xor(first_irrep, second_irrep)
    combined = jnp.bitwise_xor(
        jnp.bitwise_xor(pair_sym[:, None, None], irrep_rows[None, :, None]),
        vir_irrep[None, None, :],
    )
    allowed = combined == 0
    denominator = (
        energy_rows[None, :, None] + vir_energy[None, None, :] - pair_energy[:, None, None]
    )
    return jnp.where(allowed, numerator / denominator, jnp.float32(0.0))


def solution(mesh):
    return jax.shard_map(
        per_device,
        mesh=mesh,
        in_specs=(P("occ", "vir", None), P("vir", None, None), P(), P(), P(), P(), P()),
        out_specs=P("occ", "vir", None),
        check_vma=False,
    )
```

```python
import functools

import jax
import jax.numpy as jnp
from jax import lax
from jax.experimental import pallas as pl
from jax.experimental.pallas import tpu as pltpu
from jax.sharding import PartitionSpec as P

GROUP_ROWS = 256
VMEM_MIB = 8


def dot_nt(left, right):
    return lax.dot_general(left, right, (((1,), (1,)), ((), ())), preferred_element_type=jnp.float32)


def ladder_kernel(distances, kept_count, has_sums, loads, factor_ref, *refs):
    block_count = len(distances)
    vir_index = lax.axis_index("vir")
    z_index = vir_index // 2
    x_index = vir_index % 2
    z_low = z_index % 2
    pair_refs, refs = refs[: 2 * block_count], refs[2 * block_count :]
    before_refs = ()
    if has_sums:
        before_refs, refs = refs[:2], refs[2:]
    sent_x_ref, sent_z_ref, left_ref, right_ref = refs[:4]
    refs = refs[4:]
    loading = []
    if loads:
        source_ref, factor_ref, factor_sem, refs = factor_ref, refs[0], refs[2], refs[1:2]
        for q in range(factor_ref.shape[0]):
            loading.append(pltpu.make_async_copy(source_ref.at[q], factor_ref.at[q], factor_sem.at[q]))
            loading[q].start()
    (rows_ref,) = refs
    factor_count, size, _ = factor_ref.shape
    half = pair_refs[0].shape[0]
    width = block_count * GROUP_ROWS
    middle = size // 2

    for block in range(block_count):
        first = block * GROUP_ROWS + x_index * half
        second = block * GROUP_ROWS + (1 - x_index) * half
        rows_ref[pl.ds(pl.multiple_of(first, half), half), :] = pair_refs[2 * block][...]
        rows_ref[pl.ds(pl.multiple_of(second, half), half), :] = pair_refs[2 * block + 1][...]

    for q in range(factor_count):
        if loads:
            loading[q].wait()
        if block_count == 1:
            halves = dot_nt(rows_ref[...], factor_ref[q]).T.astype(jnp.bfloat16)
        else:
            halves = dot_nt(factor_ref[q], rows_ref[...]).astype(jnp.bfloat16)
        for block in range(block_count):
            column = pl.multiple_of((z_index ^ distances[block]) * GROUP_ROWS, GROUP_ROWS)
            taken = factor_ref[q, :, pl.ds(column, GROUP_ROWS)]
            made = halves[:, block * GROUP_ROWS : (block + 1) * GROUP_ROWS]
            target = pl.ds(q * width + block * GROUP_ROWS, GROUP_ROWS)
            left, right = (taken, made) if block < kept_count else (made, taken)
            for start in range(0, size, 2 * half):
                low, high = right[start : start + half], right[start + half : start + 2 * half]
                first = start // middle * middle + start % middle // 2
                right_ref[pl.ds(first, half), target] = jnp.where(x_index == 0, low, high)
                right_ref[pl.ds(first + GROUP_ROWS, half), target] = jnp.where(x_index == 0, high, low)
            for start in range(0, size, 2 * GROUP_ROWS):
                low = left[start : start + GROUP_ROWS]
                high = left[start + GROUP_ROWS : start + 2 * GROUP_ROWS]
                left_ref[pl.ds(start // 2, GROUP_ROWS), target] = jnp.where(z_low == 0, low, high)
                left_ref[pl.ds(middle + start // 2, GROUP_ROWS), target] = jnp.where(z_low == 0, high, low)

    products = (
        dot_nt(right_ref[pl.ds(GROUP_ROWS, GROUP_ROWS), :], left_ref[...]),
        dot_nt(right_ref[pl.ds(middle, middle), :], left_ref[pl.ds(middle, middle), :]),
    )
    for number, out_ref in enumerate((sent_x_ref, sent_z_ref)):
        product = products[number]
        if has_sums:
            product = product + before_refs[number][...]
        out_ref[...] = product.astype(out_ref.dtype)


def ladder(distances, factors, kept, swapped, sums=None, loads=False, last=False):
    factor_count, size, _ = factors.shape
    pairs = list(kept) + list(swapped)
    width = len(pairs) * GROUP_ROWS
    depth = factor_count * width
    middle = size // 2
    whole = pl.BlockSpec(memory_space=pltpu.VMEM)
    operands = [factors] + [half_block for pair in pairs for half_block in pair]
    aliases = {}
    if sums is not None:
        if not last:
            aliases = {len(operands): 0, len(operands) + 1: 1}
        operands += list(sums)
    in_specs = [whole] * len(operands)
    kind = jnp.bfloat16 if last else jnp.float32
    out_shape = [jax.ShapeDtypeStruct(shape, kind) for shape in ((GROUP_ROWS, size), (middle, middle))]
    out_shape += [jax.ShapeDtypeStruct((size, depth), jnp.bfloat16)] * 2
    scratch = [
        pltpu.VMEM((width, size), jnp.bfloat16),
    ]
    if loads:
        operands[0] = pltpu.with_memory_space_constraint(factors, pltpu.HBM)
        in_specs[0] = pl.BlockSpec(memory_space=pl.ANY)
        out_shape.append(jax.ShapeDtypeStruct(factors.shape, factors.dtype))
        scratch.append(pltpu.SemaphoreType.DMA((factor_count,)))
    out = pl.pallas_call(
        functools.partial(ladder_kernel, distances, len(kept), sums is not None, loads),
        out_shape=out_shape,
        in_specs=in_specs,
        out_specs=[whole] * len(out_shape),
        scratch_shapes=scratch,
        input_output_aliases=aliases,
        compiler_params=pltpu.CompilerParams(vmem_limit_bytes=VMEM_MIB * 1024 * 1024),
        cost_estimate=pl.CostEstimate(
            flops=(0 if loads else 3) * factor_count * width * size * size,
            bytes_accessed=2 * factor_count * size * size + 4 * size * size + 2 * width * size,
            transcendentals=0,
        ),
    )(*operands)
    return out[:2], tuple(out[2:4]), out[4:]


def keep_kernel(count, *refs):
    parts, (keep_x_ref, keep_z_ref) = refs[: 2 * count], refs[2 * count :]
    middle = keep_z_ref.shape[0]
    totals = [None, None]
    for part in range(count):
        left_ref, right_ref = parts[2 * part], parts[2 * part + 1]
        products = (
            dot_nt(right_ref[pl.ds(0, GROUP_ROWS), :], left_ref[...]),
            dot_nt(right_ref[pl.ds(middle, middle), :], left_ref[pl.ds(0, middle), :]),
        )
        totals = [p if t is None else t + p for t, p in zip(totals, products)]
    keep_x_ref[...] = totals[0]
    keep_z_ref[...] = totals[1]


def keep_sums(parts):
    size = parts[0][0].shape[0]
    middle = size // 2
    operands = [array for part in parts for array in part]
    whole = pl.BlockSpec(memory_space=pltpu.VMEM)
    return pl.pallas_call(
        functools.partial(keep_kernel, len(parts)),
        out_shape=[jax.ShapeDtypeStruct(shape, jnp.float32) for shape in ((GROUP_ROWS, size), (middle, middle))],
        in_specs=[whole] * len(operands),
        out_specs=[whole] * 2,
        compiler_params=pltpu.CompilerParams(vmem_limit_bytes=VMEM_MIB * 1024 * 1024),
        cost_estimate=pl.CostEstimate(
            flops=4 * middle * middle * sum(part[0].shape[1] for part in parts),
            bytes_accessed=2 * sum(array.size for array in operands) + 8 * middle * middle,
            transcendentals=0,
        ),
    )(*operands)


def per_device(amplitudes, factors, occ_energy, vir_energy, occ_irrep, vir_irrep, pair_orbitals):
    local_pairs, row_count, size = amplitudes.shape
    occ_total = occ_energy.shape[0]
    occ_devices = lax.axis_size("occ")
    vir_devices = lax.axis_size("vir")
    inner = GROUP_ROWS // row_count
    outer = vir_devices // inner
    assert local_pairs == 2 and outer == 4 and inner * row_count == GROUP_ROWS
    occ_index = lax.axis_index("occ")
    vir_index = lax.axis_index("vir")
    z_index = vir_index // inner
    x_index = vir_index % inner
    side = occ_index // (occ_devices // 2)
    across = occ_devices // 2

    def z_swap(block, distance):
        route = [(i, (i // inner ^ distance) * inner + i % inner) for i in range(vir_devices)]
        return lax.ppermute(block, "vir", route)

    def y_swap(block):
        return lax.ppermute(block, "occ", [(i, (i + across) % occ_devices) for i in range(occ_devices)])

    inner_groups = [[g * inner + i for i in range(inner)] for g in range(outer)]

    def x_swap(block):
        return lax.ppermute(block, "vir", [(i, i ^ 1) for i in range(vir_devices)])

    def x_pair(block):
        return block, x_swap(block)

    def x_scatter(sums):
        return lax.psum_scatter(sums, "vir", scatter_dimension=1, axis_index_groups=inner_groups)

    def z_scatter(sums, axis, distance, bit):
        sent = lax.dynamic_index_in_dim(sums, 1 - bit, axis, keepdims=False).astype(jnp.bfloat16)
        own = lax.dynamic_index_in_dim(sums, bit, axis, keepdims=False)
        return own + z_swap(sent, distance).astype(jnp.float32)

    z_high = z_index // 2
    z_low = z_index % 2

    kept_0 = lax.dynamic_index_in_dim(amplitudes, side, 0, keepdims=False)
    given = lax.dynamic_index_in_dim(amplitudes, 1 - side, 0, keepdims=False)
    swapped_0 = y_swap(given)
    def step(distance, kept, swapped, total):
        return ladder((distance,), inner, factors, kept, swapped, total)

    after = lax.optimization_barrier
    def gated(block, part):
        return after((block, part[0]))[0]

    middle = size // 2
    if inner == 2:
        kept_1 = z_swap(kept_0, 1)
        kept_pair_0 = x_pair(kept_0)
        kept_2 = z_swap(kept_0, 2)
        swapped_2 = z_swap(swapped_0, 2)
        swapped_1 = z_swap(swapped_0, 1)
        swapped_pair_0 = x_pair(swapped_0)
        kept_pair_1 = x_pair(kept_1)
        sums, part_0, (factors,) = ladder((0,), factors, [kept_pair_0], [], loads=True)
        kept_2, swapped_1, sums = after((kept_2, swapped_1, sums))
        kept_3 = z_swap(kept_2, 1)
        kept_pair_2 = x_pair(kept_2)
        swapped_pair_1 = x_pair(swapped_1)
        sums, part_1, _ = ladder((1, 0), factors, [kept_pair_1], [swapped_pair_0], sums)
        swapped_3 = z_swap(gated(swapped_2, part_0), 1)
        swapped_pair_2 = x_pair(gated(swapped_2, part_1))
        kept_pair_3 = (kept_3, z_swap(gated(kept_pair_2[1], part_1), 1))
        sums, part_2, _ = ladder((2, 1), factors, [kept_pair_2], [swapped_pair_1], sums)
        swapped_pair_3 = x_pair(gated(swapped_3, part_2))
        sums, part_3, _ = ladder((3, 2), factors, [kept_pair_3], [swapped_pair_2], sums)
        sent, part_4, _ = ladder((3,), factors, [], [swapped_pair_3], sums, last=True)
        keep_x, keep_z = keep_sums([part_0, part_1, part_2, part_3, part_4])
        came_x = x_swap(sent[0])
        came_z = z_swap(sent[1], 1)

        def added(own, came):
            return own + came.astype(jnp.float32)

        def high_half(block, index):
            return jnp.where(index == 0, block[:, :GROUP_ROWS], block[:, GROUP_ROWS:])

        first = added(keep_x[:, :middle], came_x[:, :middle])
        leaving = added(keep_x[:, middle:], came_x[:, middle:]).astype(jnp.bfloat16)
        left = added(first, z_swap(leaving, 1))
        first = added(keep_z[:GROUP_ROWS], came_z[:GROUP_ROWS])
        leaving = added(keep_z[GROUP_ROWS:], came_z[GROUP_ROWS:]).astype(jnp.bfloat16)
        right = added(first, x_swap(leaving))
        left = added(
            high_half(left, z_high), z_swap(high_half(left, 1 - z_high).astype(jnp.bfloat16), 2)
        )
        right = added(
            high_half(right, z_high), z_swap(high_half(right, 1 - z_high).astype(jnp.bfloat16), 2)
        )
        turned = jnp.concatenate([left, right], axis=0)
        own_half = jnp.where(x_index == 0, turned[:, :row_count], turned[:, row_count:])
        other_half = jnp.concatenate(
            [
                x_swap(jnp.where(x_index == 0, part[:, row_count:], part[:, :row_count]))
                for part in (left, right)
            ],
            axis=0,
        )
        by_x = jnp.stack(
            [jnp.where(x_index == 0, own_half, other_half), jnp.where(x_index == 0, other_half, own_half)]
        ).reshape(2, 4, row_count, row_count)
        own_rows = jnp.transpose(by_x, (3, 1, 0, 2)).reshape(row_count, size)
        turned = turned.astype(jnp.bfloat16).reshape(4, row_count, GROUP_ROWS)
    else:
        kept_all = lax.all_gather(kept_0, "vir", axis=0, tiled=True)
        swapped_all = lax.all_gather(swapped_0, "vir", axis=0, tiled=True)
        kept_halves = jnp.einsum("cd,qbd->qcb", kept_all, factors, preferred_element_type=jnp.float32)
        swapped_halves = jnp.einsum("cd,qad->qca", swapped_all, factors, preferred_element_type=jnp.float32)
        total = jnp.einsum(
            "qac,qcb->ab", factors, kept_halves.astype(jnp.bfloat16), preferred_element_type=jnp.float32
        ) + jnp.einsum(
            "qca,qbc->ab", swapped_halves.astype(jnp.bfloat16), factors, preferred_element_type=jnp.float32
        )
        left = x_scatter(total[:, :middle].reshape(4, inner, row_count, middle))
        left = z_scatter(left.reshape(2, 2, row_count, middle), 1, 1, z_low)
        right = z_scatter(total[:, middle:].reshape(2, 2, GROUP_ROWS, middle), 1, 1, z_low)
        right = x_scatter(right.reshape(2, inner, row_count, middle))
        own_rows = jnp.concatenate([z_scatter(left, 0, 2, z_high), z_scatter(right, 0, 2, z_high)], axis=1)
        packed = own_rows.astype(jnp.bfloat16).reshape(row_count, vir_devices, row_count)
        packed = jnp.transpose(packed, (1, 2, 0))
    if inner == 2:
        def picked(blocks):
            blocks = [jnp.where(z_low == 1, blocks[k ^ 1], blocks[k]) for k in range(4)]
            return [jnp.where(z_high == 1, blocks[k ^ 2], blocks[k]) for k in range(4)]

        turned = picked([turned[k] for k in range(4)])
        came = []
        for step in range(4):
            route = [
                (o * vir_devices + i, ((o + across) % occ_devices) * vir_devices + (i ^ 2 * step))
                for o in range(occ_devices)
                for i in range(vir_devices)
            ]
            leaving = turned[step]
            if step == 1:
                leaving = after((leaving, other_half))[0]
            came.append(lax.ppermute(leaving, ("occ", "vir"), route))
        partner = jnp.concatenate(picked(came), axis=1).astype(jnp.float32)
    else:
        partner = y_swap(lax.all_to_all(packed, "vir", 0, 0))
        partner = jnp.transpose(partner, (1, 0, 2)).reshape(row_count, size).astype(jnp.float32)

    first = jnp.where(side == 0, own_rows, partner)
    second = jnp.where(side == 0, partner, own_rows)
    numerator = jnp.stack([first, second])

    if inner == 2:
        small = (occ_energy, vir_energy, occ_irrep, vir_irrep, pair_orbitals)
        small = after((*small, part_4[0]))[:5]
        occ_energy, vir_energy, occ_irrep, vir_irrep, pair_orbitals = small
    pair_ids = lax.dynamic_slice_in_dim(pair_orbitals, occ_index * local_pairs, local_pairs, 0)
    row_start = vir_index * row_count
    energy_rows = lax.dynamic_slice_in_dim(vir_energy, row_start, row_count, 0)
    irrep_rows = lax.dynamic_slice_in_dim(vir_irrep, row_start, row_count, 0)
    positions = jnp.arange(occ_total, dtype=jnp.int32)
    first_hot = positions[None, :] == pair_ids[:, 0:1]
    second_hot = positions[None, :] == pair_ids[:, 1:2]
    pair_energy = jnp.sum(jnp.where(first_hot, occ_energy[None, :], 0.0), axis=1) + jnp.sum(
        jnp.where(second_hot, occ_energy[None, :], 0.0), axis=1
    )
    first_irrep = jnp.sum(jnp.where(first_hot, occ_irrep[None, :], 0), axis=1)
    second_irrep = jnp.sum(jnp.where(second_hot, occ_irrep[None, :], 0), axis=1)
    pair_sym = jnp.bitwise_xor(first_irrep, second_irrep)
    combined = jnp.bitwise_xor(
        jnp.bitwise_xor(pair_sym[:, None, None], irrep_rows[None, :, None]),
        vir_irrep[None, None, :],
    )
    allowed = combined == 0
    denominator = (
        energy_rows[None, :, None] + vir_energy[None, None, :] - pair_energy[:, None, None]
    )
    return jnp.where(allowed, numerator / denominator, jnp.float32(0.0))


def solution(mesh):
    return jax.shard_map(
        per_device,
        mesh=mesh,
        in_specs=(P("occ", "vir", None), P("vir", None, None), P(), P(), P(), P(), P()),
        out_specs=P("occ", "vir", None),
        check_vma=False,
    )
```

```python
import functools

import jax
import jax.numpy as jnp
from jax import lax
from jax.experimental import pallas as pl
from jax.experimental.pallas import tpu as pltpu
from jax.sharding import PartitionSpec as P

GROUP_ROWS = 256
VMEM_MIB = 8


def dot_nt(left, right):
    return lax.dot_general(left, right, (((1,), (1,)), ((), ())), preferred_element_type=jnp.float32)


def ladder_kernel(distances, kept_count, has_sums, loads, factor_ref, *refs):
    block_count = len(distances)
    vir_index = lax.axis_index("vir")
    z_index = vir_index // 2
    x_index = vir_index % 2
    z_low = z_index % 2
    pair_refs, refs = refs[: 2 * block_count], refs[2 * block_count :]
    before_refs = ()
    if has_sums:
        before_refs, refs = refs[:2], refs[2:]
    sent_x_ref, sent_z_ref, left_ref, right_ref = refs[:4]
    refs = refs[4:]
    loading = []
    if loads:
        source_ref, factor_ref, factor_sem, refs = factor_ref, refs[0], refs[2], refs[1:2]
        for q in range(factor_ref.shape[0]):
            loading.append(pltpu.make_async_copy(source_ref.at[q], factor_ref.at[q], factor_sem.at[q]))
            loading[q].start()
    (rows_ref,) = refs
    factor_count, size, _ = factor_ref.shape
    half = pair_refs[0].shape[0]
    width = block_count * GROUP_ROWS
    middle = size // 2

    for block in range(block_count):
        first = block * GROUP_ROWS + x_index * half
        second = block * GROUP_ROWS + (1 - x_index) * half
        rows_ref[pl.ds(pl.multiple_of(first, half), half), :] = pair_refs[2 * block][...]
        rows_ref[pl.ds(pl.multiple_of(second, half), half), :] = pair_refs[2 * block + 1][...]

    for q in range(factor_count):
        if loads:
            loading[q].wait()
        if block_count == 1:
            halves = dot_nt(rows_ref[...], factor_ref[q]).T.astype(jnp.bfloat16)
        else:
            halves = dot_nt(factor_ref[q], rows_ref[...]).astype(jnp.bfloat16)
        for block in range(block_count):
            column = pl.multiple_of((z_index ^ distances[block]) * GROUP_ROWS, GROUP_ROWS)
            taken = factor_ref[q, :, pl.ds(column, GROUP_ROWS)]
            made = halves[:, block * GROUP_ROWS : (block + 1) * GROUP_ROWS]
            target = pl.ds(q * width + block * GROUP_ROWS, GROUP_ROWS)
            left, right = (taken, made) if block < kept_count else (made, taken)
            for start in range(0, size, 2 * half):
                low, high = right[start : start + half], right[start + half : start + 2 * half]
                first = start // middle * middle + start % middle // 2
                right_ref[pl.ds(first, half), target] = jnp.where(x_index == 0, low, high)
                right_ref[pl.ds(first + GROUP_ROWS, half), target] = jnp.where(x_index == 0, high, low)
            for start in range(0, size, 2 * GROUP_ROWS):
                low = left[start : start + GROUP_ROWS]
                high = left[start + GROUP_ROWS : start + 2 * GROUP_ROWS]
                left_ref[pl.ds(start // 2, GROUP_ROWS), target] = jnp.where(z_low == 0, low, high)
                left_ref[pl.ds(middle + start // 2, GROUP_ROWS), target] = jnp.where(z_low == 0, high, low)

    products = (
        dot_nt(right_ref[pl.ds(GROUP_ROWS, GROUP_ROWS), :], left_ref[...]),
        dot_nt(right_ref[pl.ds(middle, middle), :], left_ref[pl.ds(middle, middle), :]),
    )
    for number, out_ref in enumerate((sent_x_ref, sent_z_ref)):
        product = products[number]
        if has_sums:
            product = product + before_refs[number][...]
        out_ref[...] = product.astype(out_ref.dtype)


def ladder(distances, factors, kept, swapped, sums=None, loads=False, last=False):
    factor_count, size, _ = factors.shape
    pairs = list(kept) + list(swapped)
    width = len(pairs) * GROUP_ROWS
    depth = factor_count * width
    middle = size // 2
    whole = pl.BlockSpec(memory_space=pltpu.VMEM)
    operands = [factors] + [half_block for pair in pairs for half_block in pair]
    aliases = {}
    if sums is not None:
        if not last:
            aliases = {len(operands): 0, len(operands) + 1: 1}
        operands += list(sums)
    in_specs = [whole] * len(operands)
    kind = jnp.bfloat16 if last else jnp.float32
    out_shape = [jax.ShapeDtypeStruct(shape, kind) for shape in ((GROUP_ROWS, size), (middle, middle))]
    out_shape += [jax.ShapeDtypeStruct((size, depth), jnp.bfloat16)] * 2
    scratch = [
        pltpu.VMEM((width, size), jnp.bfloat16),
    ]
    if loads:
        operands[0] = pltpu.with_memory_space_constraint(factors, pltpu.HBM)
        in_specs[0] = pl.BlockSpec(memory_space=pl.ANY)
        out_shape.append(jax.ShapeDtypeStruct(factors.shape, factors.dtype))
        scratch.append(pltpu.SemaphoreType.DMA((factor_count,)))
    out = pl.pallas_call(
        functools.partial(ladder_kernel, distances, len(kept), sums is not None, loads),
        out_shape=out_shape,
        in_specs=in_specs,
        out_specs=[whole] * len(out_shape),
        scratch_shapes=scratch,
        input_output_aliases=aliases,
        compiler_params=pltpu.CompilerParams(vmem_limit_bytes=VMEM_MIB * 1024 * 1024),
        cost_estimate=pl.CostEstimate(
            flops=(1 if loads else 2) * factor_count * width * size * size,
            bytes_accessed=2 * factor_count * size * size + 4 * size * size + 2 * width * size,
            transcendentals=0,
        ),
    )(*operands)
    return out[:2], tuple(out[2:4]), out[4:]


def keep_kernel(count, *refs):
    parts, (keep_x_ref, keep_z_ref) = refs[: 2 * count], refs[2 * count :]
    middle = keep_z_ref.shape[0]
    totals = [None, None]
    for part in range(count):
        left_ref, right_ref = parts[2 * part], parts[2 * part + 1]
        products = (
            dot_nt(right_ref[pl.ds(0, GROUP_ROWS), :], left_ref[...]),
            dot_nt(right_ref[pl.ds(middle, middle), :], left_ref[pl.ds(0, middle), :]),
        )
        totals = [p if t is None else t + p for t, p in zip(totals, products)]
    keep_x_ref[...] = totals[0]
    keep_z_ref[...] = totals[1]


def keep_sums(parts):
    size = parts[0][0].shape[0]
    middle = size // 2
    operands = [array for part in parts for array in part]
    whole = pl.BlockSpec(memory_space=pltpu.VMEM)
    return pl.pallas_call(
        functools.partial(keep_kernel, len(parts)),
        out_shape=[jax.ShapeDtypeStruct(shape, jnp.float32) for shape in ((GROUP_ROWS, size), (middle, middle))],
        in_specs=[whole] * len(operands),
        out_specs=[whole] * 2,
        compiler_params=pltpu.CompilerParams(vmem_limit_bytes=VMEM_MIB * 1024 * 1024),
        cost_estimate=pl.CostEstimate(
            flops=4 * middle * middle * sum(part[0].shape[1] for part in parts),
            bytes_accessed=2 * sum(array.size for array in operands) + 8 * middle * middle,
            transcendentals=0,
        ),
    )(*operands)


def per_device(amplitudes, factors, occ_energy, vir_energy, occ_irrep, vir_irrep, pair_orbitals):
    local_pairs, row_count, size = amplitudes.shape
    occ_total = occ_energy.shape[0]
    occ_devices = lax.axis_size("occ")
    vir_devices = lax.axis_size("vir")
    inner = GROUP_ROWS // row_count
    outer = vir_devices // inner
    assert local_pairs == 2 and outer == 4 and inner * row_count == GROUP_ROWS
    occ_index = lax.axis_index("occ")
    vir_index = lax.axis_index("vir")
    z_index = vir_index // inner
    x_index = vir_index % inner
    side = occ_index // (occ_devices // 2)
    across = occ_devices // 2

    def z_swap(block, distance):
        route = [(i, (i // inner ^ distance) * inner + i % inner) for i in range(vir_devices)]
        return lax.ppermute(block, "vir", route)

    def y_swap(block):
        return lax.ppermute(block, "occ", [(i, (i + across) % occ_devices) for i in range(occ_devices)])

    inner_groups = [[g * inner + i for i in range(inner)] for g in range(outer)]

    def x_swap(block):
        return lax.ppermute(block, "vir", [(i, i ^ 1) for i in range(vir_devices)])

    def x_pair(block):
        return block, x_swap(block)

    def x_scatter(sums):
        return lax.psum_scatter(sums, "vir", scatter_dimension=1, axis_index_groups=inner_groups)

    def z_scatter(sums, axis, distance, bit):
        sent = lax.dynamic_index_in_dim(sums, 1 - bit, axis, keepdims=False).astype(jnp.bfloat16)
        own = lax.dynamic_index_in_dim(sums, bit, axis, keepdims=False)
        return own + z_swap(sent, distance).astype(jnp.float32)

    z_high = z_index // 2
    z_low = z_index % 2

    kept_0 = lax.dynamic_index_in_dim(amplitudes, side, 0, keepdims=False)
    given = lax.dynamic_index_in_dim(amplitudes, 1 - side, 0, keepdims=False)
    swapped_0 = y_swap(given)
    def step(distance, kept, swapped, total):
        return ladder((distance,), inner, factors, kept, swapped, total)

    after = lax.optimization_barrier
    def gated(block, part):
        return after((block, part[0]))[0]

    middle = size // 2
    if inner == 2:
        kept_1 = z_swap(kept_0, 1)
        kept_pair_0 = x_pair(kept_0)
        kept_2 = z_swap(kept_0, 2)
        swapped_2 = z_swap(swapped_0, 2)
        swapped_1 = z_swap(swapped_0, 1)
        swapped_pair_0 = x_pair(swapped_0)
        kept_pair_1 = x_pair(kept_1)
        sums, part_0, (factors,) = ladder((0,), factors, [kept_pair_0], [], loads=True)
        kept_2, swapped_1, sums = after((kept_2, swapped_1, sums))
        kept_3 = z_swap(kept_2, 1)
        kept_pair_2 = x_pair(kept_2)
        swapped_pair_1 = x_pair(swapped_1)
        sums, part_1, _ = ladder((1, 0), factors, [kept_pair_1], [swapped_pair_0], sums)
        swapped_3 = z_swap(gated(swapped_2, part_0), 1)
        swapped_pair_2 = x_pair(gated(swapped_2, part_1))
        kept_pair_3 = (kept_3, z_swap(gated(kept_pair_2[1], part_1), 1))
        sums, part_2, _ = ladder((2, 1), factors, [kept_pair_2], [swapped_pair_1], sums)
        swapped_pair_3 = x_pair(gated(swapped_3, part_2))
        sums, part_3, _ = ladder((3, 2), factors, [kept_pair_3], [swapped_pair_2], sums)
        sent, part_4, _ = ladder((3,), factors, [], [swapped_pair_3], sums, last=True)
        keep_x, keep_z = keep_sums([part_0, part_1, part_2, part_3, part_4])
        came_x = x_swap(sent[0])
        came_z = z_swap(sent[1], 1)

        def added(own, came):
            return own + came.astype(jnp.float32)

        def high_half(block, index):
            return jnp.where(index == 0, block[:, :GROUP_ROWS], block[:, GROUP_ROWS:])

        first = added(keep_x[:, :middle], came_x[:, :middle])
        leaving = added(keep_x[:, middle:], came_x[:, middle:]).astype(jnp.bfloat16)
        left = added(first, z_swap(leaving, 1))
        first = added(keep_z[:GROUP_ROWS], came_z[:GROUP_ROWS])
        leaving = added(keep_z[GROUP_ROWS:], came_z[GROUP_ROWS:]).astype(jnp.bfloat16)
        right = added(first, x_swap(leaving))
        left = added(
            high_half(left, z_high), z_swap(high_half(left, 1 - z_high).astype(jnp.bfloat16), 2)
        )
        right = added(
            high_half(right, z_high), z_swap(high_half(right, 1 - z_high).astype(jnp.bfloat16), 2)
        )
        turned = jnp.concatenate([left, right], axis=0)
        own_half = jnp.where(x_index == 0, turned[:, :row_count], turned[:, row_count:])
        other_half = jnp.concatenate(
            [
                x_swap(
                    jnp.where(x_index == 0, part[:, row_count:], part[:, :row_count]).astype(jnp.bfloat16)
                ).astype(jnp.float32)
                for part in (left, right)
            ],
            axis=0,
        )
        by_x = jnp.stack(
            [jnp.where(x_index == 0, own_half, other_half), jnp.where(x_index == 0, other_half, own_half)]
        ).reshape(2, 4, row_count, row_count)
        own_rows = jnp.transpose(by_x, (3, 1, 0, 2)).reshape(row_count, size)
        turned = turned.astype(jnp.bfloat16).reshape(4, row_count, GROUP_ROWS)
    else:
        kept_all = lax.all_gather(kept_0, "vir", axis=0, tiled=True)
        swapped_all = lax.all_gather(swapped_0, "vir", axis=0, tiled=True)
        kept_halves = jnp.einsum("cd,qbd->qcb", kept_all, factors, preferred_element_type=jnp.float32)
        swapped_halves = jnp.einsum("cd,qad->qca", swapped_all, factors, preferred_element_type=jnp.float32)
        total = jnp.einsum(
            "qac,qcb->ab", factors, kept_halves.astype(jnp.bfloat16), preferred_element_type=jnp.float32
        ) + jnp.einsum(
            "qca,qbc->ab", swapped_halves.astype(jnp.bfloat16), factors, preferred_element_type=jnp.float32
        )
        left = x_scatter(total[:, :middle].reshape(4, inner, row_count, middle))
        left = z_scatter(left.reshape(2, 2, row_count, middle), 1, 1, z_low)
        right = z_scatter(total[:, middle:].reshape(2, 2, GROUP_ROWS, middle), 1, 1, z_low)
        right = x_scatter(right.reshape(2, inner, row_count, middle))
        own_rows = jnp.concatenate([z_scatter(left, 0, 2, z_high), z_scatter(right, 0, 2, z_high)], axis=1)
        packed = own_rows.astype(jnp.bfloat16).reshape(row_count, vir_devices, row_count)
        packed = jnp.transpose(packed, (1, 2, 0))
    if inner == 2:
        def picked(blocks):
            blocks = [jnp.where(z_low == 1, blocks[k ^ 1], blocks[k]) for k in range(4)]
            return [jnp.where(z_high == 1, blocks[k ^ 2], blocks[k]) for k in range(4)]

        turned = picked([turned[k] for k in range(4)])
        came = []
        for step in range(4):
            route = [
                (o * vir_devices + i, ((o + across) % occ_devices) * vir_devices + (i ^ 2 * step))
                for o in range(occ_devices)
                for i in range(vir_devices)
            ]
            leaving = turned[step]
            if step == 1:
                leaving = after((leaving, other_half))[0]
            came.append(lax.ppermute(leaving, ("occ", "vir"), route))
        partner = jnp.concatenate(picked(came), axis=1).astype(jnp.float32)
    else:
        partner = y_swap(lax.all_to_all(packed, "vir", 0, 0))
        partner = jnp.transpose(partner, (1, 0, 2)).reshape(row_count, size).astype(jnp.float32)

    first = jnp.where(side == 0, own_rows, partner)
    second = jnp.where(side == 0, partner, own_rows)
    numerator = jnp.stack([first, second])

    if inner == 2:
        small = (occ_energy, vir_energy, occ_irrep, vir_irrep, pair_orbitals)
        small = after((*small, part_4[0]))[:5]
        occ_energy, vir_energy, occ_irrep, vir_irrep, pair_orbitals = small
    pair_ids = lax.dynamic_slice_in_dim(pair_orbitals, occ_index * local_pairs, local_pairs, 0)
    row_start = vir_index * row_count
    energy_rows = lax.dynamic_slice_in_dim(vir_energy, row_start, row_count, 0)
    irrep_rows = lax.dynamic_slice_in_dim(vir_irrep, row_start, row_count, 0)
    positions = jnp.arange(occ_total, dtype=jnp.int32)
    first_hot = positions[None, :] == pair_ids[:, 0:1]
    second_hot = positions[None, :] == pair_ids[:, 1:2]
    pair_energy = jnp.sum(jnp.where(first_hot, occ_energy[None, :], 0.0), axis=1) + jnp.sum(
        jnp.where(second_hot, occ_energy[None, :], 0.0), axis=1
    )
    first_irrep = jnp.sum(jnp.where(first_hot, occ_irrep[None, :], 0), axis=1)
    second_irrep = jnp.sum(jnp.where(second_hot, occ_irrep[None, :], 0), axis=1)
    pair_sym = jnp.bitwise_xor(first_irrep, second_irrep)
    combined = jnp.bitwise_xor(
        jnp.bitwise_xor(pair_sym[:, None, None], irrep_rows[None, :, None]),
        vir_irrep[None, None, :],
    )
    allowed = combined == 0
    denominator = (
        energy_rows[None, :, None] + vir_energy[None, None, :] - pair_energy[:, None, None]
    )
    return jnp.where(allowed, numerator / denominator, jnp.float32(0.0))


def solution(mesh):
    return jax.shard_map(
        per_device,
        mesh=mesh,
        in_specs=(P("occ", "vir", None), P("vir", None, None), P(), P(), P(), P(), P()),
        out_specs=P("occ", "vir", None),
        check_vma=False,
    )
```

```python
import functools

import jax
import jax.numpy as jnp
from jax import lax
from jax.experimental import pallas as pl
from jax.experimental.pallas import tpu as pltpu
from jax.sharding import PartitionSpec as P

GROUP_ROWS = 256
VMEM_MIB = 8


def dot_nt(left, right):
    return lax.dot_general(left, right, (((1,), (1,)), ((), ())), preferred_element_type=jnp.float32)


def ladder_kernel(distances, kept_count, has_sums, loads, factor_ref, *refs):
    block_count = len(distances)
    vir_index = lax.axis_index("vir")
    z_index = vir_index // 2
    x_index = vir_index % 2
    z_low = z_index % 2
    pair_refs, refs = refs[: 2 * block_count], refs[2 * block_count :]
    before_refs = ()
    if has_sums:
        before_refs, refs = refs[:2], refs[2:]
    sent_x_ref, sent_z_ref, left_ref, right_ref = refs[:4]
    refs = refs[4:]
    loading = []
    if loads:
        source_ref, factor_ref, factor_sem, refs = factor_ref, refs[0], refs[2], refs[1:2]
        for q in range(factor_ref.shape[0]):
            loading.append(pltpu.make_async_copy(source_ref.at[q], factor_ref.at[q], factor_sem.at[q]))
            loading[q].start()
    (rows_ref,) = refs
    factor_count, size, _ = factor_ref.shape
    half = pair_refs[0].shape[0]
    width = block_count * GROUP_ROWS
    middle = size // 2

    for block in range(block_count):
        first = block * GROUP_ROWS + x_index * half
        second = block * GROUP_ROWS + (1 - x_index) * half
        rows_ref[pl.ds(pl.multiple_of(first, half), half), :] = pair_refs[2 * block][...]
        rows_ref[pl.ds(pl.multiple_of(second, half), half), :] = pair_refs[2 * block + 1][...]

    for q in range(factor_count):
        if loads:
            loading[q].wait()
        if block_count == 1:
            halves = dot_nt(rows_ref[...], factor_ref[q]).T.astype(jnp.bfloat16)
        else:
            halves = dot_nt(factor_ref[q], rows_ref[...]).astype(jnp.bfloat16)
        for block in range(block_count):
            column = pl.multiple_of((z_index ^ distances[block]) * GROUP_ROWS, GROUP_ROWS)
            taken = factor_ref[q, :, pl.ds(column, GROUP_ROWS)]
            made = halves[:, block * GROUP_ROWS : (block + 1) * GROUP_ROWS]
            target = pl.ds(q * width + block * GROUP_ROWS, GROUP_ROWS)
            left, right = (taken, made) if block < kept_count else (made, taken)
            for start in range(0, size, 2 * half):
                low, high = right[start : start + half], right[start + half : start + 2 * half]
                first = start // middle * middle + start % middle // 2
                right_ref[pl.ds(first, half), target] = jnp.where(x_index == 0, low, high)
                right_ref[pl.ds(first + GROUP_ROWS, half), target] = jnp.where(x_index == 0, high, low)
            for start in range(0, size, 2 * GROUP_ROWS):
                low = left[start : start + GROUP_ROWS]
                high = left[start + GROUP_ROWS : start + 2 * GROUP_ROWS]
                left_ref[pl.ds(start // 2, GROUP_ROWS), target] = jnp.where(z_low == 0, low, high)
                left_ref[pl.ds(middle + start // 2, GROUP_ROWS), target] = jnp.where(z_low == 0, high, low)

    products = (
        dot_nt(right_ref[pl.ds(GROUP_ROWS, GROUP_ROWS), :], left_ref[...]),
        dot_nt(right_ref[pl.ds(middle, middle), :], left_ref[pl.ds(middle, middle), :]),
    )
    for number, out_ref in enumerate((sent_x_ref, sent_z_ref)):
        product = products[number]
        if has_sums:
            product = product + before_refs[number][...]
        out_ref[...] = product.astype(out_ref.dtype)


def ladder(distances, factors, kept, swapped, sums=None, loads=False, last=False):
    factor_count, size, _ = factors.shape
    pairs = list(kept) + list(swapped)
    width = len(pairs) * GROUP_ROWS
    depth = factor_count * width
    middle = size // 2
    whole = pl.BlockSpec(memory_space=pltpu.VMEM)
    operands = [factors] + [half_block for pair in pairs for half_block in pair]
    aliases = {}
    if sums is not None:
        if not last:
            aliases = {len(operands): 0, len(operands) + 1: 1}
        operands += list(sums)
    in_specs = [whole] * len(operands)
    kind = jnp.bfloat16 if last else jnp.float32
    out_shape = [jax.ShapeDtypeStruct(shape, kind) for shape in ((GROUP_ROWS, size), (middle, middle))]
    out_shape += [jax.ShapeDtypeStruct((size, depth), jnp.bfloat16)] * 2
    scratch = [
        pltpu.VMEM((width, size), jnp.bfloat16),
    ]
    if loads:
        operands[0] = pltpu.with_memory_space_constraint(factors, pltpu.HBM)
        in_specs[0] = pl.BlockSpec(memory_space=pl.ANY)
        out_shape.append(jax.ShapeDtypeStruct(factors.shape, factors.dtype))
        scratch.append(pltpu.SemaphoreType.DMA((factor_count,)))
    out = pl.pallas_call(
        functools.partial(ladder_kernel, distances, len(kept), sums is not None, loads),
        out_shape=out_shape,
        in_specs=in_specs,
        out_specs=[whole] * len(out_shape),
        scratch_shapes=scratch,
        input_output_aliases=aliases,
        compiler_params=pltpu.CompilerParams(vmem_limit_bytes=VMEM_MIB * 1024 * 1024),
        cost_estimate=pl.CostEstimate(
            flops=(0 if loads else 3) * factor_count * width * size * size,
            bytes_accessed=2 * factor_count * size * size + 4 * size * size + 2 * width * size,
            transcendentals=0,
        ),
    )(*operands)
    return out[:2], tuple(out[2:4]), out[4:]


def keep_kernel(count, *refs):
    parts, (keep_x_ref, keep_z_ref) = refs[: 2 * count], refs[2 * count :]
    middle = keep_z_ref.shape[0]
    totals = [None, None]
    for part in range(count):
        left_ref, right_ref = parts[2 * part], parts[2 * part + 1]
        products = (
            dot_nt(right_ref[pl.ds(0, GROUP_ROWS), :], left_ref[...]),
            dot_nt(right_ref[pl.ds(middle, middle), :], left_ref[pl.ds(0, middle), :]),
        )
        totals = [p if t is None else t + p for t, p in zip(totals, products)]
    keep_x_ref[...] = totals[0]
    keep_z_ref[...] = totals[1]


def keep_sums(parts):
    size = parts[0][0].shape[0]
    middle = size // 2
    operands = [array for part in parts for array in part]
    whole = pl.BlockSpec(memory_space=pltpu.VMEM)
    return pl.pallas_call(
        functools.partial(keep_kernel, len(parts)),
        out_shape=[jax.ShapeDtypeStruct(shape, jnp.float32) for shape in ((GROUP_ROWS, size), (middle, middle))],
        in_specs=[whole] * len(operands),
        out_specs=[whole] * 2,
        compiler_params=pltpu.CompilerParams(vmem_limit_bytes=VMEM_MIB * 1024 * 1024),
        cost_estimate=pl.CostEstimate(
            flops=4 * middle * middle * sum(part[0].shape[1] for part in parts),
            bytes_accessed=2 * sum(array.size for array in operands) + 8 * middle * middle,
            transcendentals=0,
        ),
    )(*operands)


def per_device(amplitudes, factors, occ_energy, vir_energy, occ_irrep, vir_irrep, pair_orbitals):
    local_pairs, row_count, size = amplitudes.shape
    occ_total = occ_energy.shape[0]
    occ_devices = lax.axis_size("occ")
    vir_devices = lax.axis_size("vir")
    inner = GROUP_ROWS // row_count
    outer = vir_devices // inner
    assert local_pairs == 2 and outer == 4 and inner * row_count == GROUP_ROWS
    occ_index = lax.axis_index("occ")
    vir_index = lax.axis_index("vir")
    z_index = vir_index // inner
    x_index = vir_index % inner
    side = occ_index // (occ_devices // 2)
    across = occ_devices // 2

    def z_swap(block, distance):
        route = [(i, (i // inner ^ distance) * inner + i % inner) for i in range(vir_devices)]
        return lax.ppermute(block, "vir", route)

    def y_swap(block):
        return lax.ppermute(block, "occ", [(i, (i + across) % occ_devices) for i in range(occ_devices)])

    inner_groups = [[g * inner + i for i in range(inner)] for g in range(outer)]

    def x_swap(block):
        return lax.ppermute(block, "vir", [(i, i ^ 1) for i in range(vir_devices)])

    def x_pair(block):
        return block, x_swap(block)

    def x_scatter(sums):
        return lax.psum_scatter(sums, "vir", scatter_dimension=1, axis_index_groups=inner_groups)

    def z_scatter(sums, axis, distance, bit):
        sent = lax.dynamic_index_in_dim(sums, 1 - bit, axis, keepdims=False).astype(jnp.bfloat16)
        own = lax.dynamic_index_in_dim(sums, bit, axis, keepdims=False)
        return own + z_swap(sent, distance).astype(jnp.float32)

    z_high = z_index // 2
    z_low = z_index % 2

    kept_0 = lax.dynamic_index_in_dim(amplitudes, side, 0, keepdims=False)
    given = lax.dynamic_index_in_dim(amplitudes, 1 - side, 0, keepdims=False)
    swapped_0 = y_swap(given)
    def step(distance, kept, swapped, total):
        return ladder((distance,), inner, factors, kept, swapped, total)

    after = lax.optimization_barrier
    def gated(block, part):
        return after((block, part[0]))[0]

    middle = size // 2
    if inner == 2:
        kept_1 = z_swap(kept_0, 1)
        kept_pair_0 = x_pair(kept_0)
        kept_2 = z_swap(kept_0, 2)
        swapped_2 = z_swap(swapped_0, 2)
        swapped_1 = z_swap(swapped_0, 1)
        swapped_pair_0 = x_pair(swapped_0)
        kept_pair_1 = x_pair(kept_1)
        sums, part_0, (factors,) = ladder((0,), factors, [kept_pair_0], [], loads=True)
        kept_2, swapped_1, sums = after((kept_2, swapped_1, sums))
        kept_3 = z_swap(kept_2, 1)
        kept_pair_2 = x_pair(kept_2)
        swapped_pair_1 = x_pair(swapped_1)
        sums, part_1, _ = ladder((1, 0), factors, [kept_pair_1], [swapped_pair_0], sums)
        swapped_3 = z_swap(gated(swapped_2, part_0), 1)
        swapped_pair_2 = x_pair(gated(swapped_2, part_1))
        kept_pair_3 = (kept_3, z_swap(gated(kept_pair_2[1], part_1), 1))
        sums, part_2, _ = ladder((2, 1), factors, [kept_pair_2], [swapped_pair_1], sums)
        swapped_pair_3 = x_pair(gated(swapped_3, part_2))
        sums, part_3, _ = ladder((3, 2), factors, [kept_pair_3], [swapped_pair_2], sums)
        sent, part_4, _ = ladder((3,), factors, [], [swapped_pair_3], sums, last=True)
        keep_x, keep_z = keep_sums([part_0, part_1, part_2, part_3, part_4])
        came_x = x_swap(sent[0])
        came_z = z_swap(sent[1], 1)

        def added(own, came):
            return own + came.astype(jnp.float32)

        def high_half(block, index):
            return jnp.where(index == 0, block[:, :GROUP_ROWS], block[:, GROUP_ROWS:])

        first = added(keep_x[:, :middle], came_x[:, :middle])
        leaving = added(keep_x[:, middle:], came_x[:, middle:]).astype(jnp.bfloat16)
        left = added(first, z_swap(leaving, 1))
        first = added(keep_z[:GROUP_ROWS], came_z[:GROUP_ROWS])
        leaving = added(keep_z[GROUP_ROWS:], came_z[GROUP_ROWS:]).astype(jnp.bfloat16)
        right = added(first, x_swap(leaving))
        left = added(
            high_half(left, z_high), z_swap(high_half(left, 1 - z_high).astype(jnp.bfloat16), 2)
        )
        right = added(
            high_half(right, z_high), z_swap(high_half(right, 1 - z_high).astype(jnp.bfloat16), 2)
        )
        turned = jnp.concatenate([left, right], axis=0)
        own_half = jnp.where(x_index == 0, turned[:, :row_count], turned[:, row_count:])
        other_half = jnp.concatenate(
            [
                x_swap(jnp.where(x_index == 0, part[:, row_count:], part[:, :row_count]))
                for part in (left, right)
            ],
            axis=0,
        )
        by_x = jnp.stack(
            [jnp.where(x_index == 0, own_half, other_half), jnp.where(x_index == 0, other_half, own_half)]
        ).reshape(2, 4, row_count, row_count)
        own_rows = jnp.transpose(by_x, (3, 1, 0, 2)).reshape(row_count, size)
        turned = turned.astype(jnp.bfloat16).reshape(4, row_count, GROUP_ROWS)
    else:
        kept_all = lax.all_gather(kept_0, "vir", axis=0, tiled=True)
        swapped_all = lax.all_gather(swapped_0, "vir", axis=0, tiled=True)
        kept_halves = jnp.einsum("cd,qbd->qcb", kept_all, factors, preferred_element_type=jnp.float32)
        swapped_halves = jnp.einsum("cd,qad->qca", swapped_all, factors, preferred_element_type=jnp.float32)
        total = jnp.einsum(
            "qac,qcb->ab", factors, kept_halves.astype(jnp.bfloat16), preferred_element_type=jnp.float32
        ) + jnp.einsum(
            "qca,qbc->ab", swapped_halves.astype(jnp.bfloat16), factors, preferred_element_type=jnp.float32
        )
        left = x_scatter(total[:, :middle].reshape(4, inner, row_count, middle))
        left = z_scatter(left.reshape(2, 2, row_count, middle), 1, 1, z_low)
        right = z_scatter(total[:, middle:].reshape(2, 2, GROUP_ROWS, middle), 1, 1, z_low)
        right = x_scatter(right.reshape(2, inner, row_count, middle))
        own_rows = jnp.concatenate([z_scatter(left, 0, 2, z_high), z_scatter(right, 0, 2, z_high)], axis=1)
        packed = own_rows.astype(jnp.bfloat16).reshape(row_count, vir_devices, row_count)
        packed = jnp.transpose(packed, (1, 2, 0))
    if inner == 2:
        def picked(blocks):
            blocks = [jnp.where(z_low == 1, blocks[k ^ 1], blocks[k]) for k in range(4)]
            return [jnp.where(z_high == 1, blocks[k ^ 2], blocks[k]) for k in range(4)]

        turned = picked([turned[k] for k in range(4)])
        came = []
        for step in range(4):
            route = [
                (o * vir_devices + i, ((o + across) % occ_devices) * vir_devices + (i ^ 2 * step))
                for o in range(occ_devices)
                for i in range(vir_devices)
            ]
            leaving = turned[step]
            if step == 1:
                leaving = after((leaving, other_half[:GROUP_ROWS]))[0]
            came.append(lax.ppermute(leaving, ("occ", "vir"), route))
        partner = jnp.concatenate(picked(came), axis=1).astype(jnp.float32)
    else:
        partner = y_swap(lax.all_to_all(packed, "vir", 0, 0))
        partner = jnp.transpose(partner, (1, 0, 2)).reshape(row_count, size).astype(jnp.float32)

    first = jnp.where(side == 0, own_rows, partner)
    second = jnp.where(side == 0, partner, own_rows)
    numerator = jnp.stack([first, second])

    if inner == 2:
        small = (occ_energy, vir_energy, occ_irrep, vir_irrep, pair_orbitals)
        small = after((*small, part_4[0]))[:5]
        occ_energy, vir_energy, occ_irrep, vir_irrep, pair_orbitals = small
    pair_ids = lax.dynamic_slice_in_dim(pair_orbitals, occ_index * local_pairs, local_pairs, 0)
    row_start = vir_index * row_count
    energy_rows = lax.dynamic_slice_in_dim(vir_energy, row_start, row_count, 0)
    irrep_rows = lax.dynamic_slice_in_dim(vir_irrep, row_start, row_count, 0)
    positions = jnp.arange(occ_total, dtype=jnp.int32)
    first_hot = positions[None, :] == pair_ids[:, 0:1]
    second_hot = positions[None, :] == pair_ids[:, 1:2]
    pair_energy = jnp.sum(jnp.where(first_hot, occ_energy[None, :], 0.0), axis=1) + jnp.sum(
        jnp.where(second_hot, occ_energy[None, :], 0.0), axis=1
    )
    first_irrep = jnp.sum(jnp.where(first_hot, occ_irrep[None, :], 0), axis=1)
    second_irrep = jnp.sum(jnp.where(second_hot, occ_irrep[None, :], 0), axis=1)
    pair_sym = jnp.bitwise_xor(first_irrep, second_irrep)
    combined = jnp.bitwise_xor(
        jnp.bitwise_xor(pair_sym[:, None, None], irrep_rows[None, :, None]),
        vir_irrep[None, None, :],
    )
    allowed = combined == 0
    denominator = (
        energy_rows[None, :, None] + vir_energy[None, None, :] - pair_energy[:, None, None]
    )
    return jnp.where(allowed, numerator / denominator, jnp.float32(0.0))


def solution(mesh):
    return jax.shard_map(
        per_device,
        mesh=mesh,
        in_specs=(P("occ", "vir", None), P("vir", None, None), P(), P(), P(), P(), P()),
        out_specs=P("occ", "vir", None),
        check_vma=False,
    )
```
